256 devices in a mesh: gx: 16 (over x, y), gy: 16 (over z, core).
Axes of the slice: x: 4, y: 4, z: 8, core: 2. Of those that a mesh axis runs over, the one named last changes fastest.
Arguments:
- conserved_states: float32 [5, 256, 512, 128], P(None, 'gx', 'gy'), may hold values from -400 to 400
- thermal_level: float32 [256, 512, 128], P('gx', 'gy'), may hold values from 0.8 to 2.5
- spread_factors: float32 [5], replicated, may hold values from 0.5 to 2
Outputs:
- new_fields: float32 [5, 256, 512, 128], P(None, 'gx', 'gy')
The draws below stay inside these ranges and needn't reach their ends.
All inputs are finite; a program needn't handle non-finite values.
Results may differ from the reference program's by a relative error of at most 0.0003.
Values sent between devices are 32-bit elements; how exact they have to be, the bound alone decides.
A program may use at most 128 MiB of HBM per device.

```python
import math
import jax
import jax.numpy as jnp
from jax import lax

FIELDS = 5
SPANWISE_COUNT = 128
STREAMWISE_COUNT = 256
WALLNORMAL_COUNT = 512


def draw_conserved_states(key, part):
    key = jax.random.fold_in(key, 11)
    shape = (FIELDS, STREAMWISE_COUNT, WALLNORMAL_COUNT, SPANWISE_COUNT)
    values = 100.0 * jnp.clip(jax.random.normal(key, shape, jnp.float32), -4.0, 4.0)
    return values.astype(jnp.float32)


def levels(rng, extent, cuts, smallest, high):
    level, own = 1.0, jax.random.fold_in(rng, 6)
    for axis_at, parts in cuts:
        draws = jnp.exp(jax.random.uniform(jax.random.fold_in(own, axis_at), (parts,), jnp.float32, smallest / len(cuts), high / len(cuts)))
        level = level * jnp.repeat(draws, extent[axis_at] // parts).reshape([-1 if axis == axis_at else 1 for axis in range(len(extent))])
    return level


def setup_inputs(seed: int = 0) -> dict:
    key_list = jax.random.split(jax.random.key(seed), 4)
    conserved_states = draw_conserved_states(jax.random.fold_in(key_list[3], 71), 0)
    thermal_level = jnp.clip(0.8 + 1.7 * jax.random.uniform(key_list[1], (STREAMWISE_COUNT, WALLNORMAL_COUNT, SPANWISE_COUNT), jnp.float32) ** levels(key_list[1], (STREAMWISE_COUNT, WALLNORMAL_COUNT, SPANWISE_COUNT), ((0, 16), (1, 16)), -0.2, 0.2), 0.8, 2.5)
    spread_factors = jnp.clip(jnp.exp(jax.random.uniform(key_list[2], (FIELDS,), jnp.float32, math.log(0.5), math.log(2.0))), 0.5, 2.0)
    return {"conserved_states": conserved_states, "thermal_level": thermal_level, "spread_factors": spread_factors}


step_ratio = 5000.0
power_rule_mu = 0.7


def face_means(implicit_friction_advance, axis_number):
    moved = jnp.moveaxis(implicit_friction_advance, axis_number, 0)
    padded = jnp.concatenate([moved[:1], moved, moved[-1:]], axis=0)
    return 0.5 * (padded[:-1] + padded[1:])


def thomas(lower_diagonal, main_diag, super_diag, source):
    def forward(state_now, items):
        upper_prev, value_prev = state_now
        low_item, main_item, upper_item, source_item = items
        pivots = main_item - low_item * upper_prev
        upper_next = upper_item / pivots
        value_next = (source_item - low_item * value_prev) / pivots
        return (upper_next, value_next), (upper_next, value_next)

    start_state = (jnp.zeros_like(lower_diagonal[0]), jnp.zeros_like(source[0]))
    unused, (uppers, values) = lax.scan(forward, start_state, (lower_diagonal, main_diag, super_diag, source))

    def backward(later_value, items):
        upper_item, value_entry = items
        current = value_entry - upper_item * later_value
        return current, current

    unused_last, solved = lax.scan(backward, jnp.zeros_like(source[0]), (uppers, values), reverse=True)
    return solved


def line_solve(moved_fields, faces, spread_factors):
    weights = step_ratio * spread_factors[None, :, None, None] * faces[:, None]
    lower_diagonal = -weights[:-1]
    super_diag = -weights[1:]
    main_diag = 1.0 + weights[:-1] + weights[1:]
    return thomas(lower_diagonal, main_diag, super_diag, moved_fields)


def reference(conserved_states, thermal_level, spread_factors):
    implicit_friction_advance = thermal_level ** power_rule_mu
    moved = jnp.moveaxis(conserved_states, 1, 0)
    half_step = line_solve(moved, face_means(implicit_friction_advance, 0), spread_factors)
    across = jnp.transpose(half_step, (2, 1, 0, 3))
    solved = line_solve(across, face_means(implicit_friction_advance, 1), spread_factors)
    return jnp.transpose(solved, (1, 2, 0, 3))
```

```python
import jax
import jax.numpy as jnp
from jax import lax
from jax.experimental import pallas as pl
from jax.experimental.pallas import tpu as pltpu
from jax.sharding import PartitionSpec as P

MESH = pl.DeviceIdType.MESH
FIELDS, NX, NY, LANES = 5, 16, 32, 128
PEERS = 16
ROWS = NX * NY
XM, XR, XV, YM, YR, YV = range(6)
SHARE = {XM: 40, XR: 24, XV: 24, YM: 24, YR: 16, YV: 16}


def ring(step, size):
    return min(step, size - step)


X_STEPS = sorted(
    [(a, b) for a in range(4) for b in range(4) if (a, b) != (0, 0)],
    key=lambda s: -(ring(s[0], 4) + ring(s[1], 4)),
)
Y_STEPS = sorted(
    [(a, b) for a in range(8) for b in range(2) if (a, b) != (0, 0)],
    key=lambda s: -ring(s[0], 8),
)


def partners(axis, gx, gy):
    if axis == "gx":
        a, b = gx // 4, gx % 4
        return [(((a + i) % 4) * 4 + (b + j) % 4, gy) for i, j in X_STEPS]
    a, b = gy // 2, gy % 2
    return [(gx, ((a + i) % 8) * 2 + (b + j) % 2) for i, j in Y_STEPS]


def rows(start, count):
    return pl.ds(start, count)


def chain_matrix(mass, link, wall_low, wall_high, half):
    sides = []
    last = 2 * half - 1
    for low in (True, False):
        at = (lambda j: j) if low else (lambda j: last - j)
        edge = (lambda j: link(j)) if low else (lambda j: link(last - j - 1))
        m = mass(at(0)) + (wall_low if low else wall_high)
        steps = []
        for j in range(half - 1):
            e = edge(j)
            p = 1.0 / (m + e)
            h = e * p
            steps.append((p, h))
            m = mass(at(j + 1)) + h * m
        sides.append((steps, m))
    w = link(half - 1)
    m_low, m_high = sides[0][1], sides[1][1]
    inverse = 1.0 / (m_low * m_high + w * (m_low + m_high))
    middle = ((m_high + w) * inverse, w * inverse, (m_low + w) * inverse)
    return sides[0][0], sides[1][0], middle


def chain_solve(parts, right, half):
    low, high, (a, b, c) = parts
    last = 2 * half - 1
    ends, kept = [], []
    for steps, at in ((low, lambda j: j), (high, lambda j: last - j)):
        r = right(at(0))
        q = []
        for j, (p, h) in enumerate(steps):
            q.append(p * r)
            r = right(at(j + 1)) + h * r
        ends.append(r)
        kept.append(q)
    values = [None] * (2 * half)
    values[half - 1] = a * ends[0] + b * ends[1]
    values[half] = b * ends[0] + c * ends[1]
    for j in range(half - 2, -1, -1):
        values[j] = kept[0][j] + low[j][1] * values[j + 1]
        values[last - j] = kept[1][j] + high[j][1] * values[last - j - 1]
    return values


def kernel(
    fields_hbm, level_hbm, spread, out,
    field, level, visc, xg, xh, xq, xa, xb, xp, half, yg, yh, yq, ya, yb, yp,
    s_xm, s_xr, s_xv, s_ym, s_yr, s_yv, r_xm, r_xr, r_xv, r_ym, r_yr, r_yv,
    chain_p, chain_h, send_sem, recv_sem, in_sem,
):
    gx, gy = lax.axis_index("gx"), lax.axis_index("gy")
    sends = (s_xm, s_xr, s_xv, s_ym, s_yr, s_yv)
    recvs = (r_xm, r_xr, r_xv, r_ym, r_yr, r_yv)
    everyone = partners("gx", gx, gy) + partners("gy", gx, gy)

    barrier = pltpu.get_barrier_semaphore()
    for device in everyone:
        pl.semaphore_signal(barrier, inc=1, device_id=device, device_id_type=MESH)
    level_in = pltpu.make_async_copy(level_hbm, level, in_sem.at[0])
    fields_in = pltpu.make_async_copy(fields_hbm, field, in_sem.at[1])
    level_in.start()
    fields_in.start()

    def axis_of(what):
        return "gx" if what in (XM, XR, XV) else "gy"

    def send(what):
        axis, size = axis_of(what), SHARE[what]
        me = gx if axis == "gx" else gy
        for device in partners(axis, gx, gy):
            peer = device[0] if axis == "gx" else device[1]
            pltpu.make_async_remote_copy(
                src_ref=sends[what].at[rows(pl.multiple_of(peer * size, 8), size)],
                dst_ref=recvs[what].at[rows(pl.multiple_of(me * size, 8), size)],
                send_sem=send_sem.at[what],
                recv_sem=recv_sem.at[what],
                device_id=device,
                device_id_type=MESH,
            ).start()
        mine = rows(pl.multiple_of(me * size, 8), size)
        recvs[what][mine] = sends[what][mine]

    def total(what):
        part = rows(0, (PEERS - 1) * SHARE[what])
        return pltpu.make_async_remote_copy(
            src_ref=sends[what].at[part],
            dst_ref=recvs[what].at[part],
            send_sem=send_sem.at[what],
            recv_sem=recv_sem.at[what],
            device_id=everyone[0],
            device_id_type=MESH,
        )

    rate = [2500.0 * spread[f] for f in range(FIELDS)]
    zero = jnp.zeros((16, LANES), jnp.float32)
    one = jnp.ones((16, LANES), jnp.float32)

    for ref, size, used in ((s_xm, 40, 34), (s_xr, 24, 20), (s_xv, 24, 20)):
        for row in range(used, size):
            ref[pl.ds(row, 16, stride=size)] = zero
    for ref, size, spare in ((s_ym, 24, (6, 7, 14, 15, 21, 22, 23)), (s_yr, 16, (5, 6, 7, 13, 14, 15))):
        for row in spare:
            ref[pl.ds(row, 16, stride=size)] = zero
    r_xr[rows(PEERS * SHARE[XR], 8)] = zero[:8]

    level_in.wait()

    def power(t, carry):
        at = rows(pl.multiple_of(t * 64, 64), 64)
        visc[at] = jnp.exp(0.7 * jnp.log(level[at]))
        return carry

    lax.fori_loop(0, ROWS // 64, power, 0)
    fields_in.wait()

    def x_row(f, i, s):
        return rows(pl.multiple_of(f * ROWS + i * NY + s * 16, 16), 16)

    def x_visc(i, s):
        return visc[rows(pl.multiple_of(i * NY + s * 16, 16), 16)]

    for s in range(2):
        nu0, nu1 = x_visc(0, s), x_visc(1, s)
        start = (
            nu1,
            tuple(rate[f] * (nu0 + nu1) for f in range(FIELDS)),
            (one,) * FIELDS,
            (one,) * FIELDS,
            tuple(field[x_row(f, 1, s)] for f in range(FIELDS)),
            tuple(field[x_row(f, 0, s)] for f in range(FIELDS)),
        )

        def forward(i, state, s=s):
            nu, edge, mass, first, right, first_right = state
            nu_next = x_visc(i + 1, s)
            face = nu + nu_next
            out_state = ([], [], [], [], [])
            for f in range(FIELDS):
                e, m, r = edge[f], mass[f], right[f]
                w = rate[f] * face
                p = 1.0 / (e + w + m)
                g, h = e * p, w * p
                at = x_row(f, i, s)
                xg[at] = g
                xh[at] = h
                xq[at] = p * r
                for box, item in zip(
                    out_state,
                    (g * w, 1.0 + h * m, first[f] + g * m, field[x_row(f, i + 1, s)] + h * r, first_right[f] + g * r),
                ):
                    box.append(item)
            return (nu_next,) + tuple(tuple(box) for box in out_state)

        nu, edge, mass, first, right, first_right = lax.fori_loop(1, NX - 1, forward, start)
        for f in range(FIELDS):
            for v, value in enumerate((first[f], mass[f], edge[f])):
                base = v * 8 + 2 * f + s if f < 4 else 24 + 2 * v + s
                s_xm[pl.ds(base, 16, stride=40)] = value
            for v, value in enumerate((first_right[f], right[f])):
                base = v * 8 + 2 * f + s if f < 4 else 16 + 2 * v + s
                s_xr[pl.ds(base, 16, stride=24)] = value
        s_xm[pl.ds(30 + s, 16, stride=40)] = nu0
        s_xm[pl.ds(32 + s, 16, stride=40)] = nu

    pl.semaphore_wait(barrier, len(everyone))
    send(XM)
    send(XR)

    def y_visc(j):
        return visc[pl.ds(j, 16, stride=NY)]

    def y_row(f, j):
        return rows(pl.multiple_of((f * NY + j) * 16, 16), 16)

    nu0, nu1 = y_visc(0), y_visc(1)
    start = (nu1, tuple(rate[f] * (nu0 + nu1) for f in range(FIELDS)), (one,) * FIELDS, (one,) * FIELDS)

    def forward(j, state):
        nu, edge, mass, first = state
        nu_next = y_visc(j + 1)
        face = nu + nu_next
        out_state = ([], [], [])
        for f in range(FIELDS):
            e, m = edge[f], mass[f]
            w = rate[f] * face
            p = 1.0 / (e + w + m)
            g, h = e * p, w * p
            at = y_row(f, j)
            yg[at] = g
            yh[at] = h
            yq[at] = p
            for box, item in zip(out_state, (g * w, 1.0 + h * m, first[f] + g * m)):
                box.append(item)
        return (nu_next,) + tuple(tuple(box) for box in out_state)

    nu, edge, mass, first = lax.fori_loop(1, NY - 1, forward, start)
    for f in range(FIELDS):
        for v, value in enumerate((first[f], mass[f], edge[f])):
            s_ym[pl.ds(v * 8 + f, 16, stride=24)] = value
    s_ym[pl.ds(5, 16, stride=24)] = nu0
    s_ym[pl.ds(13, 16, stride=24)] = nu
    send(YM)

    for s in range(2):
        for f in range(FIELDS):
            for i, ends in ((0, (one, zero)), (NX - 1, (zero, one))):
                at = x_row(f, i, s)
                xa[at], xb[at], xp[at] = ends[0], ends[1], zero

        def backward(k, state, s=s):
            i = NX - 2 - k
            new = []
            for f in range(FIELDS):
                a, b, p = state[f]
                at = x_row(f, i, s)
                h = xh[at]
                a, b, p = xg[at] + h * a, h * b, xq[at] + h * p
                xa[at], xb[at], xp[at] = a, b, p
                new.append((a, b, p))
            return tuple(new)

        lax.fori_loop(0, NX - 2, backward, ((zero, one, zero),) * FIELDS)

    line = lax.broadcasted_iota(jnp.int32, (16, LANES), 0)
    odd = line % 2 == 1
    rate_x = jnp.full((16, LANES), rate[FIELDS - 1], jnp.float32)
    for f in range(4):
        rate_x = jnp.where(line // 2 == f, rate[f], rate_x)

    def pack(ref, k, size, low, high):
        return jnp.concatenate([ref[rows(k * size + low, 8)], ref[rows(k * size + high, 8)]], axis=0)

    def x_mass(j):
        v = j % 2
        return pack(r_xm, j // 2, 40, 8 * v, 24 + 2 * v)

    def x_end_visc(k, v):
        base = k * 40 + 30 + 2 * v
        return jnp.where(odd, r_xm[rows(base + 1, 1)], r_xm[rows(base, 1)])

    def x_link(j):
        k = j // 2
        if j % 2 == 0:
            return pack(r_xm, k, 40, 16, 28)
        return rate_x * (x_end_visc(k, 1) + x_end_visc(k + 1, 0))

    total(XM).wait_recv()
    parts = chain_matrix(
        x_mass, x_link, 2.0 * rate_x * x_end_visc(0, 0), 2.0 * rate_x * x_end_visc(PEERS - 1, 1), PEERS
    )
    total(XR).wait_recv()
    solved = chain_solve(parts, lambda j: pack(r_xr, j // 2, 24, 8 * (j % 2), 16 + 2 * (j % 2)), PEERS)
    for k in range(PEERS):
        for v in range(2):
            s_xv[rows(k * 24 + 8 * v, 8)] = solved[2 * k + v][:8]
            s_xv[rows(k * 24 + 16 + 2 * v, 2)] = solved[2 * k + v][8:10]
    send(XV)

    def natural(f, j):
        return pl.ds(f * ROWS + j, 16, stride=NY)

    for f in range(FIELDS):
        for j, ends in ((0, (one, zero)), (NY - 1, (zero, one))):
            at = natural(f, j)
            ya[at], yb[at], yp[at] = ends[0], ends[1], zero

    def backward(k, state):
        j = NY - 2 - k
        new = []
        for f in range(FIELDS):
            a, b = state[f]
            at = y_row(f, j)
            h = yh[at]
            a, b = yg[at] + h * a, h * b
            ya[natural(f, j)], yb[natural(f, j)] = a, b
            new.append((a, b))
        return tuple(new)

    lax.fori_loop(0, NY - 2, backward, ((zero, one),) * FIELDS)

    rate_y = jnp.full((8, LANES), rate[FIELDS - 1], jnp.float32)
    line = lax.broadcasted_iota(jnp.int32, (8, LANES), 0)
    for f in range(4):
        rate_y = jnp.where(line == f, rate[f], rate_y)

    def y_end_visc(k, v):
        return r_ym[rows(k * 24 + 5 + 8 * v, 1)]

    def y_link(j):
        k = j // 2
        if j % 2 == 0:
            return r_ym[rows(k * 24 + 16, 8)]
        return rate_y * (y_end_visc(k, 1) + y_end_visc(k + 1, 0))

    total(YM).wait_recv()
    low, high, middle = chain_matrix(
        lambda j: r_ym[rows((j // 2) * 24 + 8 * (j % 2), 8)],
        y_link,
        2.0 * rate_y * y_end_visc(0, 0),
        2.0 * rate_y * y_end_visc(PEERS - 1, 1),
        PEERS,
    )
    for side, steps in enumerate((low, high)):
        for j, (p, h) in enumerate(steps):
            chain_p[rows((side * PEERS + j) * 8, 8)] = p
            chain_h[rows((side * PEERS + j) * 8, 8)] = h

    total(XV).wait_recv()
    for f in range(FIELDS):
        low_end, high_end = [], []
        for s in range(2):
            base = (2 * f + s, 8 + 2 * f + s) if f < 4 else (16 + s, 18 + s)
            low_end.append(r_xv[pl.ds(base[0], 16, stride=24)])
            high_end.append(r_xv[pl.ds(base[1], 16, stride=24)])
        low_end = jnp.concatenate(low_end, axis=0)
        high_end = jnp.concatenate(high_end, axis=0)

        def finish_x(i, carry, f=f, low_end=low_end, high_end=high_end):
            at = rows(pl.multiple_of(f * ROWS + i * NY, NY), NY)
            value = xp[at] + xa[at] * low_end + xb[at] * high_end
            half[at] = value
            s_yr[rows(i * 16 + f, 1)] = jnp.sum(ya[at] * value, axis=0, keepdims=True)
            s_yr[rows(i * 16 + 8 + f, 1)] = jnp.sum(yb[at] * value, axis=0, keepdims=True)
            return carry

        lax.fori_loop(0, NX, finish_x, 0)
    send(YR)

    def forward(j, right):
        new = []
        for f in range(FIELDS):
            at = y_row(f, j)
            yg[at] = yq[at] * right[f]
            new.append(half[natural(f, j + 1)] + yh[at] * right[f])
        return tuple(new)

    lax.fori_loop(1, NY - 1, forward, tuple(half[natural(f, 1)] for f in range(FIELDS)))

    def backward(k, state):
        j = NY - 2 - k
        new = []
        for f in range(FIELDS):
            at = y_row(f, j)
            p = yg[at] + yh[at] * state[f]
            yp[natural(f, j)] = p
            new.append(p)
        return tuple(new)

    lax.fori_loop(0, NY - 2, backward, (zero,) * FIELDS)

    total(YR).wait_recv()
    parts = tuple(
        [
            (chain_p[rows((side * PEERS + j) * 8, 8)], chain_h[rows((side * PEERS + j) * 8, 8)])
            for j in range(PEERS - 1)
        ]
        for side in range(2)
    ) + (middle,)
    solved = chain_solve(parts, lambda j: r_yr[rows((j // 2) * 16 + 8 * (j % 2), 8)], PEERS)
    for k in range(PEERS):
        for v in range(2):
            s_yv[rows(k * 16 + 8 * v, 8)] = solved[2 * k + v]
    send(YV)

    total(YV).wait_recv()

    def finish_y(i, carry):
        for f in range(FIELDS):
            at = rows(pl.multiple_of(f * ROWS + i * NY, NY), NY)
            low_end, high_end = r_yv[rows(i * 16 + f, 1)], r_yv[rows(i * 16 + 8 + f, 1)]
            out[at] = yp[at] + ya[at] * low_end + yb[at] * high_end
        return carry

    lax.fori_loop(0, NX, finish_y, 0)
    for what in range(6):
        total(what).wait_send()


def shards(conserved_states, thermal_level, spread_factors):
    def buffer(count):
        return pltpu.VMEM((count, LANES), jnp.float32)

    whole = buffer(FIELDS * ROWS)
    messages = [buffer(PEERS * SHARE[what]) for what in range(6)]
    arrivals = [buffer(PEERS * SHARE[what] + 8) for what in range(6)]
    solved = pl.pallas_call(
        kernel,
        out_shape=jax.ShapeDtypeStruct((FIELDS * ROWS, LANES), jnp.float32),
        in_specs=[
            pl.BlockSpec(memory_space=pl.ANY),
            pl.BlockSpec(memory_space=pl.ANY),
            pl.BlockSpec(memory_space=pltpu.SMEM),
        ],
        out_specs=pl.BlockSpec(memory_space=pltpu.VMEM),
        scratch_shapes=[whole, buffer(ROWS), buffer(ROWS)]
        + [whole] * 13
        + messages
        + arrivals
        + [
            buffer(2 * PEERS * 8),
            buffer(2 * PEERS * 8),
            pltpu.SemaphoreType.DMA((6,)),
            pltpu.SemaphoreType.DMA((6,)),
            pltpu.SemaphoreType.DMA((2,)),
        ],
        compiler_params=pltpu.CompilerParams(
            collective_id=0, has_side_effects=True, vmem_limit_bytes=48 * 1024 * 1024
        ),
    )(
        conserved_states.reshape(FIELDS * ROWS, LANES),
        thermal_level.reshape(ROWS, LANES),
        spread_factors,
    )
    return solved.reshape(conserved_states.shape)


def solution(mesh):
    return jax.shard_map(
        shards,
        mesh=mesh,
        in_specs=(P(None, "gx", "gy", None), P("gx", "gy", None), P()),
        out_specs=P(None, "gx", "gy", None),
        check_vma=False,
    )
```

```python
import jax
import jax.numpy as jnp
from jax import lax
from jax.experimental import pallas as pl
from jax.experimental.pallas import tpu as pltpu
from jax.sharding import PartitionSpec as P

MESH = pl.DeviceIdType.MESH
FIELDS, NX, NY, LANES = 5, 16, 32, 128
PEERS = 16
ROWS = NX * NY
XM, XR, XV, YM, YR, YV = range(6)
MESSAGES = {
    XM: ("gx", 0, 0, 40),
    XR: ("gx", 0, 40, 14),
    XV: ("gx", 1, 0, 20),
    YM: ("gy", 2, 0, 17),
    YR: ("gy", 3, 0, 10),
    YV: ("gy", 4, 0, 10),
}
SHARE = (56, 24, 24, 16, 16)

X_STEPS = (
    (2, 2), (2, 1), (1, 2), (2, 3), (3, 2), (1, 1), (1, 3), (3, 1),
    (3, 3), (0, 2), (2, 0), (0, 1), (1, 0), (0, 3), (3, 0),
)
Y_STEPS = (
    (4, 0), (4, 1), (3, 0), (3, 1), (5, 0), (5, 1), (2, 0), (2, 1),
    (6, 0), (6, 1), (1, 0), (1, 1), (7, 0), (7, 1), (0, 1),
)


def partners(axis, gx, gy):
    if axis == "gx":
        return [(((gx + 4 * i) & 12) + ((gx + j) & 3), gy) for i, j in X_STEPS]
    return [(gx, ((gy + 2 * i) & 14) + ((gy + j) & 1)) for i, j in Y_STEPS]


def rows(start, count):
    return pl.ds(start, count)


def chain_matrix(mass, link, wall_low, wall_high, half):
    sides = []
    last = 2 * half - 1
    for low in (True, False):
        at = (lambda j: j) if low else (lambda j: last - j)
        edge = (lambda j: link(j)) if low else (lambda j: link(last - j - 1))
        m = mass(at(0)) + (wall_low if low else wall_high)
        steps = []
        for j in range(half - 1):
            e = edge(j)
            p = 1.0 / (m + e)
            h = e * p
            steps.append((p, h))
            m = mass(at(j + 1)) + h * m
        sides.append((steps, m))
    w = link(half - 1)
    m_low, m_high = sides[0][1], sides[1][1]
    inverse = 1.0 / (m_low * m_high + w * (m_low + m_high))
    middle = ((m_high + w) * inverse, w * inverse, (m_low + w) * inverse)
    return sides[0][0], sides[1][0], middle


def chain_solve(parts, right, half):
    low, high, (a, b, c) = parts
    last = 2 * half - 1
    ends, kept = [], []
    for steps, at in ((low, lambda j: j), (high, lambda j: last - j)):
        r = right(at(0))
        q = []
        for j, (p, h) in enumerate(steps):
            q.append(p * r)
            r = right(at(j + 1)) + h * r
        ends.append(r)
        kept.append(q)
    values = [None] * (2 * half)
    values[half - 1] = a * ends[0] + b * ends[1]
    values[half] = b * ends[0] + c * ends[1]
    for j in range(half - 2, -1, -1):
        values[j] = kept[0][j] + low[j][1] * values[j + 1]
        values[last - j] = kept[1][j] + high[j][1] * values[last - j - 1]
    return values


def kernel(
    fields_hbm, level_hbm, spread, out,
    field, level, visc, xg, xh, xq, xa, xb, xp, half, yg, yh, yq, ya, yb, yp,
    s_x, s_xv, s_ym, s_yr, s_yv, r_x, r_xv, r_ym, r_yr, r_yv,
    chain_p, chain_h, send_sem, recv_sem, in_sem,
):
    gx, gy = lax.axis_index("gx"), lax.axis_index("gy")
    sends = (s_x, s_xv, s_ym, s_yr, s_yv)
    recvs = (r_x, r_xv, r_ym, r_yr, r_yv)
    everyone = partners("gx", gx, gy) + partners("gy", gx, gy)

    barrier = pltpu.get_barrier_semaphore()
    for device in everyone:
        pl.semaphore_signal(barrier, inc=1, device_id=device, device_id_type=MESH)
    level_in = pltpu.make_async_copy(level_hbm, level, in_sem.at[0])
    fields_in = pltpu.make_async_copy(fields_hbm, field, in_sem.at[1])
    level_in.start()
    fields_in.start()

    def send(what):
        axis, buffer, first, count = MESSAGES[what]
        size = SHARE[buffer]
        me = gx if axis == "gx" else gy
        for device in partners(axis, gx, gy):
            peer = device[0] if axis == "gx" else device[1]
            pltpu.make_async_remote_copy(
                src_ref=sends[buffer].at[rows(pl.multiple_of(peer * size, 8) + first, count)],
                dst_ref=recvs[buffer].at[rows(pl.multiple_of(me * size, 8) + first, count)],
                send_sem=send_sem.at[what],
                recv_sem=recv_sem.at[what],
                device_id=device,
                device_id_type=MESH,
            ).start()

    def keep(buffer, me):
        mine = rows(pl.multiple_of(me * SHARE[buffer], 8), SHARE[buffer])
        recvs[buffer][mine] = sends[buffer][mine]

    def total(what):
        axis, buffer, first, count = MESSAGES[what]
        part = rows(0, (PEERS - 1) * count)
        return pltpu.make_async_remote_copy(
            src_ref=sends[buffer].at[part],
            dst_ref=recvs[buffer].at[part],
            send_sem=send_sem.at[what],
            recv_sem=recv_sem.at[what],
            device_id=everyone[0],
            device_id_type=MESH,
        )

    rate = [2500.0 * spread[f] for f in range(FIELDS)]
    zero = jnp.zeros((16, LANES), jnp.float32)
    one = jnp.ones((16, LANES), jnp.float32)

    for ref, size, unused in (
        (s_x, 56, (54, 55)),
        (s_xv, 24, (20, 21, 22, 23)),
        (s_ym, 24, tuple(range(17, 24))),
        (s_yr, 16, tuple(range(10, 16))),
        (s_yv, 16, tuple(range(10, 16))),
    ):
        for row in unused:
            ref[pl.ds(row, 16, stride=size)] = zero
    for ref, size, unused in ((r_x, 56, (54, 55)), (r_ym, 24, tuple(range(17, 24))), (r_yr, 16, tuple(range(10, 16)))):
        for row in unused:
            ref[pl.ds(row, 16, stride=size)] = zero
    r_x[rows(PEERS * 56, 8)] = zero[:8]

    level_in.wait()

    def power(t, carry):
        at = rows(pl.multiple_of(t * 64, 64), 64)
        visc[at] = jnp.exp(0.7 * jnp.log(level[at]))
        return carry

    lax.fori_loop(0, ROWS // 64, power, 0)
    fields_in.wait()

    def x_row(f, i, s):
        return rows(pl.multiple_of(f * ROWS + i * NY + s * 16, 16), 16)

    def x_visc(i, s):
        return visc[rows(pl.multiple_of(i * NY + s * 16, 16), 16)]

    for s in range(2):
        nu0, nu1 = x_visc(0, s), x_visc(1, s)
        start = (
            nu1,
            tuple(rate[f] * (nu0 + nu1) for f in range(FIELDS)),
            (one,) * FIELDS,
            (one,) * FIELDS,
            tuple(field[x_row(f, 1, s)] for f in range(FIELDS)),
            tuple(field[x_row(f, 0, s)] for f in range(FIELDS)),
        )

        def forward(i, state, s=s):
            nu, edge, mass, first, right, first_right = state
            nu_next = x_visc(i + 1, s)
            face = nu + nu_next
            out_state = ([], [], [], [], [])
            for f in range(FIELDS):
                e, m, r = edge[f], mass[f], right[f]
                w = rate[f] * face
                p = 1.0 / (e + w + m)
                g, h = e * p, w * p
                at = x_row(f, i, s)
                xg[at] = g
                xh[at] = h
                xq[at] = p * r
                for box, item in zip(
                    out_state,
                    (g * w, 1.0 + h * m, first[f] + g * m, field[x_row(f, i + 1, s)] + h * r, first_right[f] + g * r),
                ):
                    box.append(item)
            return (nu_next,) + tuple(tuple(box) for box in out_state)

        nu, edge, mass, first, right, first_right = lax.fori_loop(1, NX - 1, forward, start)
        for f in range(FIELDS):
            for v, value in enumerate((first[f], mass[f], edge[f])):
                base = v * 8 + 2 * f + s if f < 4 else 24 + 2 * v + s
                s_x[pl.ds(base, 16, stride=56)] = value
            for v, value in enumerate((first_right[f], right[f])):
                base = 34 + v * 8 + 2 * f + s if f < 4 else 50 + 2 * v + s
                s_x[pl.ds(base, 16, stride=56)] = value
        s_x[pl.ds(30 + s, 16, stride=56)] = nu0
        s_x[pl.ds(32 + s, 16, stride=56)] = nu

    pl.semaphore_wait(barrier, len(everyone))
    send(XM)
    send(XR)
    keep(0, gx)

    def y_visc(j):
        return visc[pl.ds(j, 16, stride=NY)]

    def y_row(f, j):
        return rows(pl.multiple_of((f * NY + j) * 16, 16), 16)

    nu0, nu1 = y_visc(0), y_visc(1)
    start = (nu1, tuple(rate[f] * (nu0 + nu1) for f in range(FIELDS)), (one,) * FIELDS, (one,) * FIELDS)

    def forward(j, state):
        nu, edge, mass, first = state
        nu_next = y_visc(j + 1)
        face = nu + nu_next
        out_state = ([], [], [])
        for f in range(FIELDS):
            e, m = edge[f], mass[f]
            w = rate[f] * face
            p = 1.0 / (e + w + m)
            g, h = e * p, w * p
            at = y_row(f, j)
            yg[at] = g
            yh[at] = h
            yq[at] = p
            for box, item in zip(out_state, (g * w, 1.0 + h * m, first[f] + g * m)):
                box.append(item)
        return (nu_next,) + tuple(tuple(box) for box in out_state)

    nu, edge, mass, first = lax.fori_loop(1, NY - 1, forward, start)
    for f in range(FIELDS):
        for v, value in enumerate((first[f], mass[f], edge[f])):
            s_ym[pl.ds(v * 5 + f, 16, stride=24)] = value
    s_ym[pl.ds(15, 16, stride=24)] = nu0
    s_ym[pl.ds(16, 16, stride=24)] = nu
    send(YM)
    keep(2, gy)

    for s in range(2):
        for f in range(FIELDS):
            for i, ends in ((0, (one, zero)), (NX - 1, (zero, one))):
                at = x_row(f, i, s)
                xa[at], xb[at], xp[at] = ends[0], ends[1], zero

        def backward(k, state, s=s):
            i = NX - 2 - k
            new = []
            for f in range(FIELDS):
                a, b, p = state[f]
                at = x_row(f, i, s)
                h = xh[at]
                a, b, p = xg[at] + h * a, h * b, xq[at] + h * p
                xa[at], xb[at], xp[at] = a, b, p
                new.append((a, b, p))
            return tuple(new)

        lax.fori_loop(0, NX - 2, backward, ((zero, one, zero),) * FIELDS)

    line = lax.broadcasted_iota(jnp.int32, (16, LANES), 0)
    odd = line % 2 == 1
    rate_x = jnp.full((16, LANES), rate[FIELDS - 1], jnp.float32)
    for f in range(4):
        rate_x = jnp.where(line // 2 == f, rate[f], rate_x)

    def pack(ref, k, size, low, high):
        return jnp.concatenate([ref[rows(k * size + low, 8)], ref[rows(k * size + high, 8)]], axis=0)

    def x_mass(j):
        v = j % 2
        return pack(r_x, j // 2, 56, 8 * v, 24 + 2 * v)

    def x_end_visc(k, v):
        base = k * 56 + 30 + 2 * v
        return jnp.where(odd, r_x[rows(base + 1, 1)], r_x[rows(base, 1)])

    def x_link(j):
        k = j // 2
        if j % 2 == 0:
            return pack(r_x, k, 56, 16, 28)
        return rate_x * (x_end_visc(k, 1) + x_end_visc(k + 1, 0))

    total(XM).wait_recv()
    parts = chain_matrix(
        x_mass, x_link, 2.0 * rate_x * x_end_visc(0, 0), 2.0 * rate_x * x_end_visc(PEERS - 1, 1), PEERS
    )
    total(XR).wait_recv()
    solved = chain_solve(parts, lambda j: pack(r_x, j // 2, 56, 34 + 8 * (j % 2), 50 + 2 * (j % 2)), PEERS)
    for k in range(PEERS):
        for v in range(2):
            s_xv[rows(k * 24 + 8 * v, 8)] = solved[2 * k + v][:8]
            s_xv[rows(k * 24 + 16 + 2 * v, 2)] = solved[2 * k + v][8:10]
    send(XV)
    keep(1, gx)

    def natural(f, j):
        return pl.ds(f * ROWS + j, 16, stride=NY)

    for f in range(FIELDS):
        for j, ends in ((0, (one, zero)), (NY - 1, (zero, one))):
            at = natural(f, j)
            ya[at], yb[at], yp[at] = ends[0], ends[1], zero

    def backward(k, state):
        j = NY - 2 - k
        new = []
        for f in range(FIELDS):
            a, b = state[f]
            at = y_row(f, j)
            h = yh[at]
            a, b = yg[at] + h * a, h * b
            ya[natural(f, j)], yb[natural(f, j)] = a, b
            new.append((a, b))
        return tuple(new)

    lax.fori_loop(0, NY - 2, backward, ((zero, one),) * FIELDS)

    rate_y = jnp.full((8, LANES), rate[FIELDS - 1], jnp.float32)
    line = lax.broadcasted_iota(jnp.int32, (8, LANES), 0)
    for f in range(4):
        rate_y = jnp.where(line == f, rate[f], rate_y)

    def y_end_visc(k, v):
        return r_ym[rows(k * 24 + 15 + v, 1)]

    def y_link(j):
        k = j // 2
        if j % 2 == 0:
            return r_ym[rows(k * 24 + 10, 8)]
        return rate_y * (y_end_visc(k, 1) + y_end_visc(k + 1, 0))

    total(YM).wait_recv()
    low, high, middle = chain_matrix(
        lambda j: r_ym[rows((j // 2) * 24 + 5 * (j % 2), 8)],
        y_link,
        2.0 * rate_y * y_end_visc(0, 0),
        2.0 * rate_y * y_end_visc(PEERS - 1, 1),
        PEERS,
    )
    for side, steps in enumerate((low, high)):
        for j, (p, h) in enumerate(steps):
            chain_p[rows((side * PEERS + j) * 8, 8)] = p
            chain_h[rows((side * PEERS + j) * 8, 8)] = h

    total(XV).wait_recv()
    for f in range(FIELDS):
        low_end, high_end = [], []
        for s in range(2):
            base = (2 * f + s, 8 + 2 * f + s) if f < 4 else (16 + s, 18 + s)
            low_end.append(r_xv[pl.ds(base[0], 16, stride=24)])
            high_end.append(r_xv[pl.ds(base[1], 16, stride=24)])
        low_end = jnp.concatenate(low_end, axis=0)
        high_end = jnp.concatenate(high_end, axis=0)

        def finish_x(i, carry, f=f, low_end=low_end, high_end=high_end):
            at = rows(pl.multiple_of(f * ROWS + i * NY, NY), NY)
            value = xp[at] + xa[at] * low_end + xb[at] * high_end
            half[at] = value
            s_yr[rows(i * 16 + f, 1)] = jnp.sum(ya[at] * value, axis=0, keepdims=True)
            s_yr[rows(i * 16 + 5 + f, 1)] = jnp.sum(yb[at] * value, axis=0, keepdims=True)
            return carry

        lax.fori_loop(0, NX, finish_x, 0, unroll=8)
    send(YR)
    keep(3, gy)

    def forward(j, right):
        new = []
        for f in range(FIELDS):
            at = y_row(f, j)
            yg[at] = yq[at] * right[f]
            new.append(half[natural(f, j + 1)] + yh[at] * right[f])
        return tuple(new)

    lax.fori_loop(1, NY - 1, forward, tuple(half[natural(f, 1)] for f in range(FIELDS)))

    def backward(k, state):
        j = NY - 2 - k
        new = []
        for f in range(FIELDS):
            at = y_row(f, j)
            p = yg[at] + yh[at] * state[f]
            yp[natural(f, j)] = p
            new.append(p)
        return tuple(new)

    lax.fori_loop(0, NY - 2, backward, (zero,) * FIELDS)

    total(YR).wait_recv()
    parts = tuple(
        [
            (chain_p[rows((side * PEERS + j) * 8, 8)], chain_h[rows((side * PEERS + j) * 8, 8)])
            for j in range(PEERS - 1)
        ]
        for side in range(2)
    ) + (middle,)
    solved = chain_solve(parts, lambda j: r_yr[rows((j // 2) * 16 + 5 * (j % 2), 8)], PEERS)
    for k in range(PEERS):
        for v in range(2):
            s_yv[rows(k * 16 + 5 * v, 5)] = solved[2 * k + v][:5]
    send(YV)
    keep(4, gy)

    total(YV).wait_recv()

    def finish_y(i, carry):
        for f in range(FIELDS):
            at = rows(pl.multiple_of(f * ROWS + i * NY, NY), NY)
            low_end, high_end = r_yv[rows(i * 16 + f, 1)], r_yv[rows(i * 16 + 5 + f, 1)]
            out[at] = yp[at] + ya[at] * low_end + yb[at] * high_end
        return carry

    lax.fori_loop(0, NX, finish_y, 0, unroll=2)
    for what in range(6):
        total(what).wait_send()


def shards(conserved_states, thermal_level, spread_factors):
    def buffer(count):
        return pltpu.VMEM((count, LANES), jnp.float32)

    whole = buffer(FIELDS * ROWS)
    messages = [buffer(PEERS * size) for size in SHARE]
    arrivals = [buffer(PEERS * size + 8) for size in SHARE]
    solved = pl.pallas_call(
        kernel,
        out_shape=pltpu.VMEM((FIELDS * ROWS, LANES), jnp.float32),
        in_specs=[
            pl.BlockSpec(memory_space=pl.ANY),
            pl.BlockSpec(memory_space=pl.ANY),
            pl.BlockSpec(memory_space=pltpu.SMEM),
        ],
        out_specs=pl.BlockSpec(memory_space=pltpu.VMEM),
        scratch_shapes=[whole, buffer(ROWS), buffer(ROWS)]
        + [whole] * 13
        + messages
        + arrivals
        + [
            buffer(2 * PEERS * 8),
            buffer(2 * PEERS * 8),
            pltpu.SemaphoreType.DMA((6,)),
            pltpu.SemaphoreType.DMA((6,)),
            pltpu.SemaphoreType.DMA((2,)),
        ],
        compiler_params=pltpu.CompilerParams(
            collective_id=0, has_side_effects=True, vmem_limit_bytes=60 * 1024 * 1024
        ),
    )(
        conserved_states.reshape(FIELDS * ROWS, LANES),
        thermal_level.reshape(ROWS, LANES),
        spread_factors,
    )
    return solved.reshape(conserved_states.shape)


def solution(mesh):
    return jax.shard_map(
        shards,
        mesh=mesh,
        in_specs=(P(None, "gx", "gy", None), P("gx", "gy", None), P()),
        out_specs=P(None, "gx", "gy", None),
        check_vma=False,
    )
```

```python
import jax
import jax.numpy as jnp
from jax import lax
from jax.experimental import pallas as pl
from jax.experimental.pallas import tpu as pltpu
from jax.sharding import PartitionSpec as P

MESH = pl.DeviceIdType.MESH
FIELDS, NX, NY, LANES = 5, 16, 32, 128
PEERS = 16
ROWS = NX * NY
GROUPS = ((0, 1, 2), (3, 4))


def message_table():
    table = {"ym": ("gy", 3 * FIELDS + 2, 24)}
    for g, group in enumerate(GROUPS):
        n = len(group)
        for name, axis, count in (
            ("xo", "gx", 10 * n + (4 if g == 0 else 0)),
            ("xv", "gx", 4 * n),
            ("yr", "gy", 2 * n),
            ("yv", "gy", 2 * n),
        ):
            table[name, g] = (axis, count, -(-count // 8) * 8)
    return table


MESSAGES = message_table()
ORDER = {what: k for k, what in enumerate(MESSAGES)}

X_STEPS = (
    (2, 2), (2, 1), (1, 2), (2, 3), (3, 2), (1, 1), (1, 3), (3, 1),
    (3, 3), (0, 2), (2, 0), (0, 1), (1, 0), (0, 3), (3, 0),
)
Y_STEPS = (
    (4, 0), (4, 1), (3, 0), (3, 1), (5, 0), (5, 1), (2, 0), (2, 1),
    (6, 0), (6, 1), (1, 0), (1, 1), (7, 0), (7, 1), (0, 1),
)


def partners(axis, gx, gy):
    if axis == "gx":
        return [(((gx + 4 * i) & 12) + ((gx + j) & 3), gy) for i, j in X_STEPS]
    return [(gx, ((gy + 2 * i) & 14) + ((gy + j) & 1)) for i, j in Y_STEPS]


def rows(start, count):
    return pl.ds(start, count)


def chain_matrix(mass, link, wall_low, wall_high, half):
    sides = []
    last = 2 * half - 1
    for low in (True, False):
        at = (lambda j: j) if low else (lambda j: last - j)
        edge = (lambda j: link(j)) if low else (lambda j: link(last - j - 1))
        m = mass(at(0)) + (wall_low if low else wall_high)
        steps = []
        for j in range(half - 1):
            e = edge(j)
            p = 1.0 / (m + e)
            h = e * p
            steps.append((p, h))
            m = mass(at(j + 1)) + h * m
        sides.append((steps, m))
    w = link(half - 1)
    m_low, m_high = sides[0][1], sides[1][1]
    inverse = 1.0 / (m_low * m_high + w * (m_low + m_high))
    middle = ((m_high + w) * inverse, w * inverse, (m_low + w) * inverse)
    return sides[0][0], sides[1][0], middle


def chain_solve(parts, right, half):
    low, high, (a, b, c) = parts
    last = 2 * half - 1
    ends, kept = [], []
    for steps, at in ((low, lambda j: j), (high, lambda j: last - j)):
        r = right(at(0))
        q = []
        for j, (p, h) in enumerate(steps):
            q.append(p * r)
            r = right(at(j + 1)) + h * r
        ends.append(r)
        kept.append(q)
    values = [None] * (2 * half)
    values[half - 1] = a * ends[0] + b * ends[1]
    values[half] = b * ends[0] + c * ends[1]
    for j in range(half - 2, -1, -1):
        values[j] = kept[0][j] + low[j][1] * values[j + 1]
        values[last - j] = kept[1][j] + high[j][1] * values[last - j - 1]
    return values


def kernel(
    fields_hbm, level_hbm, spread, out,
    field, level, visc, xg, xh, xq, xa, xb, xp, half, yg, yh, yq, ya, yb, yp,
    *rest,
):
    gx, gy = lax.axis_index("gx"), lax.axis_index("gy")
    count = len(MESSAGES)
    sends = dict(zip(MESSAGES, rest[:count]))
    recvs = dict(zip(MESSAGES, rest[count : 2 * count]))
    chain_p, chain_h, send_sem, recv_sem, in_sem = rest[2 * count :]
    everyone = partners("gx", gx, gy) + partners("gy", gx, gy)

    barrier = pltpu.get_barrier_semaphore()
    for device in everyone:
        pl.semaphore_signal(barrier, inc=1, device_id=device, device_id_type=MESH)
    level_in = pltpu.make_async_copy(level_hbm, level, in_sem.at[0])
    fields_in = pltpu.make_async_copy(fields_hbm, field, in_sem.at[1])
    level_in.start()
    fields_in.start()

    def send(what):
        axis, count, size = MESSAGES[what]
        me = gx if axis == "gx" else gy
        for device in partners(axis, gx, gy):
            peer = device[0] if axis == "gx" else device[1]
            pltpu.make_async_remote_copy(
                src_ref=sends[what].at[rows(pl.multiple_of(peer * size, 8), count)],
                dst_ref=recvs[what].at[rows(pl.multiple_of(me * size, 8), count)],
                send_sem=send_sem.at[ORDER[what]],
                recv_sem=recv_sem.at[ORDER[what]],
                device_id=device,
                device_id_type=MESH,
            ).start()

    def keep(what):
        axis, count, size = MESSAGES[what]
        mine = rows(pl.multiple_of((gx if axis == "gx" else gy) * size, 8), size)
        recvs[what][mine] = sends[what][mine]

    def total(what):
        axis, count, size = MESSAGES[what]
        part = rows(0, (PEERS - 1) * count)
        return pltpu.make_async_remote_copy(
            src_ref=sends[what].at[part],
            dst_ref=recvs[what].at[part],
            send_sem=send_sem.at[ORDER[what]],
            recv_sem=recv_sem.at[ORDER[what]],
            device_id=everyone[0],
            device_id_type=MESH,
        )

    def share(what, row):
        return pl.ds(row, PEERS, stride=MESSAGES[what][2])

    def peer_rows(what, k, row, count=8):
        return rows(k * MESSAGES[what][2] + row, count)

    rate = [2500.0 * spread[f] for f in range(FIELDS)]
    zero = jnp.zeros((16, LANES), jnp.float32)
    one = jnp.ones((16, LANES), jnp.float32)

    for what, (axis, used, size) in MESSAGES.items():
        for row in range(used, size):
            sends[what][share(what, row)] = zero
            recvs[what][share(what, row)] = zero
        recvs[what][rows(PEERS * size, 8)] = zero[:8]

    level_in.wait()

    def power(t, carry):
        at = rows(pl.multiple_of(t * 64, 64), 64)
        visc[at] = jnp.exp(0.7 * jnp.log(level[at]))
        return carry

    lax.fori_loop(0, ROWS // 64, power, 0)
    fields_in.wait()

    def x_row(f, i, s):
        return rows(pl.multiple_of(f * ROWS + i * NY + s * 16, 16), 16)

    def x_visc(i, s):
        return visc[rows(pl.multiple_of(i * NY + s * 16, 16), 16)]

    for s in range(2):
        nu0, nu1 = x_visc(0, s), x_visc(1, s)
        start = (
            nu1,
            tuple(rate[f] * (nu0 + nu1) for f in range(FIELDS)),
            (one,) * FIELDS,
            (one,) * FIELDS,
            tuple(field[x_row(f, 1, s)] for f in range(FIELDS)),
            tuple(field[x_row(f, 0, s)] for f in range(FIELDS)),
        )

        def forward(i, state, s=s):
            nu, edge, mass, first, right, first_right = state
            nu_next = x_visc(i + 1, s)
            face = nu + nu_next
            out_state = ([], [], [], [], [])
            for f in range(FIELDS):
                e, m, r = edge[f], mass[f], right[f]
                w = rate[f] * face
                p = 1.0 / (e + w + m)
                g, h = e * p, w * p
                at = x_row(f, i, s)
                xg[at] = g
                xh[at] = h
                xq[at] = p * r
                for box, item in zip(
                    out_state,
                    (g * w, 1.0 + h * m, first[f] + g * m, field[x_row(f, i + 1, s)] + h * r, first_right[f] + g * r),
                ):
                    box.append(item)
            return (nu_next,) + tuple(tuple(box) for box in out_state)

        nu, edge, mass, first, right, first_right = lax.fori_loop(1, NX - 1, forward, start)
        for g, group in enumerate(GROUPS):
            what, n = ("xo", g), 2 * len(group)
            for place, f in enumerate(group):
                for v, value in enumerate((first[f], mass[f], edge[f], first_right[f], right[f])):
                    sends[what][share(what, v * n + 2 * place + s)] = value
        what, n = ("xo", 0), 10 * len(GROUPS[0])
        sends[what][share(what, n + s)] = nu0
        sends[what][share(what, n + 2 + s)] = nu

    pl.semaphore_wait(barrier, len(everyone))
    for g in range(len(GROUPS)):
        send(("xo", g))
    for g in range(len(GROUPS)):
        keep(("xo", g))

    def y_visc(j):
        return visc[pl.ds(j, 16, stride=NY)]

    def y_row(f, j):
        return rows(pl.multiple_of((f * NY + j) * 16, 16), 16)

    nu0, nu1 = y_visc(0), y_visc(1)
    start = (nu1, tuple(rate[f] * (nu0 + nu1) for f in range(FIELDS)), (one,) * FIELDS, (one,) * FIELDS)

    def forward(j, state):
        nu, edge, mass, first = state
        nu_next = y_visc(j + 1)
        face = nu + nu_next
        out_state = ([], [], [])
        for f in range(FIELDS):
            e, m = edge[f], mass[f]
            w = rate[f] * face
            p = 1.0 / (e + w + m)
            g, h = e * p, w * p
            at = y_row(f, j)
            yg[at] = g
            yh[at] = h
            yq[at] = p
            for box, item in zip(out_state, (g * w, 1.0 + h * m, first[f] + g * m)):
                box.append(item)
        return (nu_next,) + tuple(tuple(box) for box in out_state)

    nu, edge, mass, first = lax.fori_loop(1, NY - 1, forward, start)
    at = 0
    y_at = []
    for group in GROUPS:
        y_at.append(at)
        for v, values in enumerate((first, mass, edge)):
            for f in group:
                sends["ym"][share("ym", at)] = values[f]
                at += 1
    sends["ym"][share("ym", at)] = nu0
    sends["ym"][share("ym", at + 1)] = nu
    send("ym")
    keep("ym")

    for s in range(2):
        for f in range(FIELDS):
            for i, ends in ((0, (one, zero)), (NX - 1, (zero, one))):
                at = x_row(f, i, s)
                xa[at], xb[at], xp[at] = ends[0], ends[1], zero

        def backward(k, state, s=s):
            i = NX - 2 - k
            new = []
            for f in range(FIELDS):
                a, b, p = state[f]
                at = x_row(f, i, s)
                h = xh[at]
                a, b, p = xg[at] + h * a, h * b, xq[at] + h * p
                xa[at], xb[at], xp[at] = a, b, p
                new.append((a, b, p))
            return tuple(new)

        lax.fori_loop(0, NX - 2, backward, ((zero, one, zero),) * FIELDS)

    line = lax.broadcasted_iota(jnp.int32, (8, LANES), 0)

    def rates(group, each):
        value = jnp.full((8, LANES), rate[group[-1]], jnp.float32)
        for place, f in enumerate(group[:-1]):
            value = jnp.where(line // each == place, rate[f], value)
        return value

    for g, group in enumerate(GROUPS):
        what, n = ("xo", g), 2 * len(group)
        rate_x = rates(group, 2)

        def end_visc(k, v):
            base = 10 * len(GROUPS[0]) + 2 * v
            low, high = (recvs["xo", 0][peer_rows(("xo", 0), k, base + s, 1)] for s in range(2))
            return jnp.where(line % 2 == 1, high, low)

        def link(j):
            if j % 2 == 0:
                return recvs[what][peer_rows(what, j // 2, 2 * n)]
            return rate_x * (end_visc(j // 2, 1) + end_visc(j // 2 + 1, 0))

        total(what).wait_recv()
        parts = chain_matrix(
            lambda j: recvs[what][peer_rows(what, j // 2, n * (j % 2))],
            link,
            2.0 * rate_x * end_visc(0, 0),
            2.0 * rate_x * end_visc(PEERS - 1, 1),
            PEERS,
        )
        solved = chain_solve(parts, lambda j: recvs[what][peer_rows(what, j // 2, n * (3 + j % 2))], PEERS)
        back = ("xv", g)
        for k in range(PEERS):
            for v in range(2):
                sends[back][peer_rows(back, k, n * v, n)] = solved[2 * k + v][:n]
        send(back)
        keep(back)

    def natural(f, j):
        return pl.ds(f * ROWS + j, 16, stride=NY)

    for f in range(FIELDS):
        for j, ends in ((0, (one, zero)), (NY - 1, (zero, one))):
            at = natural(f, j)
            ya[at], yb[at], yp[at] = ends[0], ends[1], zero

    def backward(k, state):
        j = NY - 2 - k
        new = []
        for f in range(FIELDS):
            a, b = state[f]
            at = y_row(f, j)
            h = yh[at]
            a, b = yg[at] + h * a, h * b
            ya[natural(f, j)], yb[natural(f, j)] = a, b
            new.append((a, b))
        return tuple(new)

    lax.fori_loop(0, NY - 2, backward, ((zero, one),) * FIELDS)

    total("ym").wait_recv()
    middles = []
    for g, group in enumerate(GROUPS):
        n = len(group)
        rate_y = rates(group, 1)

        def end_visc(k, v):
            return recvs["ym"][peer_rows("ym", k, 3 * FIELDS + v, 1)]

        def link(j):
            if j % 2 == 0:
                return recvs["ym"][peer_rows("ym", j // 2, y_at[g] + 2 * n)]
            return rate_y * (end_visc(j // 2, 1) + end_visc(j // 2 + 1, 0))

        low, high, middle = chain_matrix(
            lambda j: recvs["ym"][peer_rows("ym", j // 2, y_at[g] + n * (j % 2))],
            link,
            2.0 * rate_y * end_visc(0, 0),
            2.0 * rate_y * end_visc(PEERS - 1, 1),
            PEERS,
        )
        middles.append(middle)
        for side, steps in enumerate((low, high)):
            for j, (p, h) in enumerate(steps):
                at = rows(((2 * g + side) * PEERS + j) * 8, 8)
                chain_p[at] = p
                chain_h[at] = h

    for g, group in enumerate(GROUPS):
        what, back, n = ("yr", g), ("xv", g), len(group)
        total(back).wait_recv()
        for place, f in enumerate(group):
            low_end, high_end = (
                jnp.concatenate(
                    [recvs[back][share(back, 2 * n * v + 2 * place + s)] for s in range(2)], axis=0
                )
                for v in range(2)
            )

            def finish_x(i, carry, f=f, place=place, low_end=low_end, high_end=high_end):
                at = rows(pl.multiple_of(f * ROWS + i * NY, NY), NY)
                value = xp[at] + xa[at] * low_end + xb[at] * high_end
                half[at] = value
                low = jnp.sum(ya[at] * value, axis=0, keepdims=True)
                high = jnp.sum(yb[at] * value, axis=0, keepdims=True)
                sends[what][peer_rows(what, i, place, 1)] = low
                sends[what][peer_rows(what, i, n + place, 1)] = high
                return carry

            lax.fori_loop(0, NX, finish_x, 0, unroll=8)
        send(what)
        keep(what)

    def forward(j, right):
        new = []
        for f in range(FIELDS):
            at = y_row(f, j)
            yg[at] = yq[at] * right[f]
            new.append(half[natural(f, j + 1)] + yh[at] * right[f])
        return tuple(new)

    lax.fori_loop(1, NY - 1, forward, tuple(half[natural(f, 1)] for f in range(FIELDS)))

    def backward(k, state):
        j = NY - 2 - k
        new = []
        for f in range(FIELDS):
            at = y_row(f, j)
            p = yg[at] + yh[at] * state[f]
            yp[natural(f, j)] = p
            new.append(p)
        return tuple(new)

    lax.fori_loop(0, NY - 2, backward, (zero,) * FIELDS)

    for g, group in enumerate(GROUPS):
        what, back, n = ("yr", g), ("yv", g), len(group)
        parts = []
        for side in range(2):
            at = [rows(((2 * g + side) * PEERS + j) * 8, 8) for j in range(PEERS - 1)]
            parts.append([(chain_p[place], chain_h[place]) for place in at])
        total(what).wait_recv()
        solved = chain_solve(
            (*parts, middles[g]), lambda j: recvs[what][peer_rows(what, j // 2, n * (j % 2))], PEERS
        )
        for k in range(PEERS):
            for v in range(2):
                sends[back][peer_rows(back, k, n * v, n)] = solved[2 * k + v][:n]
        send(back)
        keep(back)

    for g, group in enumerate(GROUPS):
        back, n = ("yv", g), len(group)
        total(back).wait_recv()

        def finish_y(i, carry):
            for place, f in enumerate(group):
                at = rows(pl.multiple_of(f * ROWS + i * NY, NY), NY)
                low_end = recvs[back][peer_rows(back, i, place, 1)]
                high_end = recvs[back][peer_rows(back, i, n + place, 1)]
                out[at] = yp[at] + ya[at] * low_end + yb[at] * high_end
            return carry

        lax.fori_loop(0, NX, finish_y, 0, unroll=2)
    for what in MESSAGES:
        total(what).wait_send()


def shards(conserved_states, thermal_level, spread_factors):
    def buffer(count):
        return pltpu.VMEM((count, LANES), jnp.float32)

    whole = buffer(FIELDS * ROWS)
    messages = [buffer(PEERS * size) for axis, count, size in MESSAGES.values()]
    arrivals = [buffer(PEERS * size + 8) for axis, count, size in MESSAGES.values()]
    solved = pl.pallas_call(
        kernel,
        out_shape=pltpu.VMEM((FIELDS * ROWS, LANES), jnp.float32),
        in_specs=[
            pl.BlockSpec(memory_space=pl.ANY),
            pl.BlockSpec(memory_space=pl.ANY),
            pl.BlockSpec(memory_space=pltpu.SMEM),
        ],
        out_specs=pl.BlockSpec(memory_space=pltpu.VMEM),
        scratch_shapes=[whole, buffer(ROWS), buffer(ROWS)]
        + [whole] * 13
        + messages
        + arrivals
        + [
            buffer(2 * len(GROUPS) * PEERS * 8),
            buffer(2 * len(GROUPS) * PEERS * 8),
            pltpu.SemaphoreType.DMA((len(MESSAGES),)),
            pltpu.SemaphoreType.DMA((len(MESSAGES),)),
            pltpu.SemaphoreType.DMA((2,)),
        ],
        compiler_params=pltpu.CompilerParams(
            collective_id=0, has_side_effects=True, vmem_limit_bytes=60 * 1024 * 1024
        ),
    )(
        conserved_states.reshape(FIELDS * ROWS, LANES),
        thermal_level.reshape(ROWS, LANES),
        spread_factors,
    )
    return solved.reshape(conserved_states.shape)


def solution(mesh):
    return jax.shard_map(
        shards,
        mesh=mesh,
        in_specs=(P(None, "gx", "gy", None), P("gx", "gy", None), P()),
        out_specs=P(None, "gx", "gy", None),
        check_vma=False,
    )
```

```python
import jax
import jax.numpy as jnp
from jax import lax
from jax.experimental import pallas as pl
from jax.experimental.pallas import tpu as pltpu
from jax.sharding import PartitionSpec as P

MESH = pl.DeviceIdType.MESH
FIELDS, NX, NY, LANES = 5, 16, 32, 128
PEERS = 16
ROWS = NX * NY
GROUPS = ((0, 1, 2), (3, 4))


def message_table():
    table = {"ym": ("gy", 3 * FIELDS + 2, 24)}
    for g, group in enumerate(GROUPS):
        n = len(group)
        for name, axis, count in (
            ("xo", "gx", 10 * n + (4 if g == 0 else 0)),
            ("xv", "gx", 4 * n),
            ("yr", "gy", 2 * n),
            ("yv", "gy", 2 * n),
        ):
            table[name, g] = (axis, count, -(-count // 8) * 8)
    return table


MESSAGES = message_table()
ORDER = {what: k for k, what in enumerate(MESSAGES)}

X_STEPS = (
    (2, 2), (2, 1), (1, 2), (2, 3), (3, 2), (1, 1), (1, 3), (3, 1),
    (3, 3), (0, 2), (2, 0), (0, 1), (1, 0), (0, 3), (3, 0),
)
Y_STEPS = (
    (4, 0), (4, 1), (3, 0), (3, 1), (5, 0), (5, 1), (2, 0), (2, 1),
    (6, 0), (6, 1), (1, 0), (1, 1), (7, 0), (7, 1), (0, 1),
)


X_FIRST = tuple(range(16))
Y_FIRST = (1, 3, 9, 5, 8, 2, 7, 11, 4, 10, 6, 13, 15, 12, 0, 14)


def ring(step, size):
    return min(step, size - step)


def others(order, me):
    place = sum(k * (me == at).astype(jnp.int32) for k, at in enumerate(order))
    return [jnp.where(place > k, order[k], order[k + 1]) for k in range(len(order) - 1)]


def partners(axis, gx, gy):
    if axis == "gx":
        return [(((gx + 4 * i) & 12) + ((gx + j) & 3), gy) for i, j in X_STEPS]
    return [(gx, ((gy + 2 * i) & 14) + ((gy + j) & 1)) for i, j in Y_STEPS]


def rows(start, count):
    return pl.ds(start, count)


def chain_matrix(mass, link, wall_low, wall_high, half):
    sides = []
    last = 2 * half - 1
    for low in (True, False):
        at = (lambda j: j) if low else (lambda j: last - j)
        edge = (lambda j: link(j)) if low else (lambda j: link(last - j - 1))
        m = mass(at(0)) + (wall_low if low else wall_high)
        steps = []
        for j in range(half - 1):
            e = edge(j)
            p = 1.0 / (m + e)
            h = e * p
            steps.append((p, h))
            m = mass(at(j + 1)) + h * m
        sides.append((steps, m))
    w = link(half - 1)
    m_low, m_high = sides[0][1], sides[1][1]
    inverse = 1.0 / (m_low * m_high + w * (m_low + m_high))
    middle = ((m_high + w) * inverse, w * inverse, (m_low + w) * inverse)
    return sides[0][0], sides[1][0], middle


def chain_solve(parts, right, half):
    low, high, (a, b, c) = parts
    last = 2 * half - 1
    ends, kept = [], []
    for steps, at in ((low, lambda j: j), (high, lambda j: last - j)):
        r = right(at(0))
        q = []
        for j, (p, h) in enumerate(steps):
            q.append(p * r)
            r = right(at(j + 1)) + h * r
        ends.append(r)
        kept.append(q)
    values = [None] * (2 * half)
    values[half - 1] = a * ends[0] + b * ends[1]
    values[half] = b * ends[0] + c * ends[1]
    for j in range(half - 2, -1, -1):
        values[j] = kept[0][j] + low[j][1] * values[j + 1]
        values[last - j] = kept[1][j] + high[j][1] * values[last - j - 1]
    return values


def kernel(
    fields_hbm, level_hbm, spread, out,
    field, level, visc, xg, xh, xq, xa, xb, xp, half, yg, yh, yq, ya, yb, yp,
    *rest,
):
    gx, gy = lax.axis_index("gx"), lax.axis_index("gy")
    count = len(MESSAGES)
    sends = dict(zip(MESSAGES, rest[:count]))
    recvs = dict(zip(MESSAGES, rest[count : 2 * count]))
    chain_p, chain_h, send_sem, recv_sem, in_sem = rest[2 * count :]
    everyone = partners("gx", gx, gy) + partners("gy", gx, gy)
    hops = [ring(i, 4) + ring(j, 4) for i, j in X_STEPS] + [ring(i, 8) for i, j in Y_STEPS]
    greeted = [everyone[k] for k in sorted(range(len(everyone)), key=lambda k: -hops[k])]

    barrier = pltpu.get_barrier_semaphore()
    for device in greeted:
        pl.semaphore_signal(barrier, inc=1, device_id=device, device_id_type=MESH)
    level_in = pltpu.make_async_copy(level_hbm, level, in_sem.at[0])
    fields_in = pltpu.make_async_copy(fields_hbm, field, in_sem.at[1])
    level_in.start()
    fields_in.start()

    x_order = [(peer, gy) for peer in others(X_FIRST, gx)]
    y_order = [(gx, peer) for peer in others(Y_FIRST, gy)]

    def send(what, devices=None):
        axis, count, size = MESSAGES[what]
        me = gx if axis == "gx" else gy
        for device in devices or partners(axis, gx, gy):
            peer = device[0] if axis == "gx" else device[1]
            pltpu.make_async_remote_copy(
                src_ref=sends[what].at[rows(pl.multiple_of(peer * size, 8), count)],
                dst_ref=recvs[what].at[rows(pl.multiple_of(me * size, 8), count)],
                send_sem=send_sem.at[ORDER[what]],
                recv_sem=recv_sem.at[ORDER[what]],
                device_id=device,
                device_id_type=MESH,
            ).start()

    def keep(what):
        axis, count, size = MESSAGES[what]
        mine = rows(pl.multiple_of((gx if axis == "gx" else gy) * size, 8), size)
        recvs[what][mine] = sends[what][mine]

    def total(what):
        axis, count, size = MESSAGES[what]
        part = rows(0, (PEERS - 1) * count)
        return pltpu.make_async_remote_copy(
            src_ref=sends[what].at[part],
            dst_ref=recvs[what].at[part],
            send_sem=send_sem.at[ORDER[what]],
            recv_sem=recv_sem.at[ORDER[what]],
            device_id=everyone[0],
            device_id_type=MESH,
        )

    def share(what, row):
        return pl.ds(row, PEERS, stride=MESSAGES[what][2])

    def peer_rows(what, k, row, count=8):
        return rows(k * MESSAGES[what][2] + row, count)

    rate = [2500.0 * spread[f] for f in range(FIELDS)]
    zero = jnp.zeros((16, LANES), jnp.float32)
    one = jnp.ones((16, LANES), jnp.float32)

    for what, (axis, used, size) in MESSAGES.items():
        for row in range(used, size):
            sends[what][share(what, row)] = zero
            recvs[what][share(what, row)] = zero
        recvs[what][rows(PEERS * size, 8)] = zero[:8]

    level_in.wait()

    def power(t, carry):
        at = rows(pl.multiple_of(t * 64, 64), 64)
        visc[at] = jnp.exp(0.7 * jnp.log(level[at]))
        return carry

    lax.fori_loop(0, ROWS // 64, power, 0)
    fields_in.wait()

    def x_row(f, i, s):
        return rows(pl.multiple_of(f * ROWS + i * NY + s * 16, 16), 16)

    def x_visc(i, s):
        return visc[rows(pl.multiple_of(i * NY + s * 16, 16), 16)]

    for s in range(2):
        nu0, nu1 = x_visc(0, s), x_visc(1, s)
        start = (
            nu1,
            tuple(rate[f] * (nu0 + nu1) for f in range(FIELDS)),
            (one,) * FIELDS,
            (one,) * FIELDS,
            tuple(field[x_row(f, 1, s)] for f in range(FIELDS)),
            tuple(field[x_row(f, 0, s)] for f in range(FIELDS)),
        )

        def forward(i, state, s=s):
            nu, edge, mass, first, right, first_right = state
            nu_next = x_visc(i + 1, s)
            face = nu + nu_next
            out_state = ([], [], [], [], [])
            for f in range(FIELDS):
                e, m, r = edge[f], mass[f], right[f]
                w = rate[f] * face
                p = 1.0 / (e + w + m)
                g, h = e * p, w * p
                at = x_row(f, i, s)
                xg[at] = g
                xh[at] = h
                xq[at] = p * r
                for box, item in zip(
                    out_state,
                    (g * w, 1.0 + h * m, first[f] + g * m, field[x_row(f, i + 1, s)] + h * r, first_right[f] + g * r),
                ):
                    box.append(item)
            return (nu_next,) + tuple(tuple(box) for box in out_state)

        nu, edge, mass, first, right, first_right = lax.fori_loop(1, NX - 1, forward, start)
        for g, group in enumerate(GROUPS):
            what, n = ("xo", g), 2 * len(group)
            for place, f in enumerate(group):
                for v, value in enumerate((first[f], mass[f], edge[f], first_right[f], right[f])):
                    sends[what][share(what, v * n + 2 * place + s)] = value
        what, n = ("xo", 0), 10 * len(GROUPS[0])
        sends[what][share(what, n + s)] = nu0
        sends[what][share(what, n + 2 + s)] = nu

    pl.semaphore_wait(barrier, len(everyone))
    for g in range(len(GROUPS)):
        send(("xo", g))
    for g in range(len(GROUPS)):
        keep(("xo", g))

    def y_visc(j):
        return visc[pl.ds(j, 16, stride=NY)]

    def y_row(f, j):
        return rows(pl.multiple_of((f * NY + j) * 16, 16), 16)

    nu0, nu1 = y_visc(0), y_visc(1)
    start = (nu1, tuple(rate[f] * (nu0 + nu1) for f in range(FIELDS)), (one,) * FIELDS, (one,) * FIELDS)

    def forward(j, state):
        nu, edge, mass, first = state
        nu_next = y_visc(j + 1)
        face = nu + nu_next
        out_state = ([], [], [])
        for f in range(FIELDS):
            e, m = edge[f], mass[f]
            w = rate[f] * face
            p = 1.0 / (e + w + m)
            g, h = e * p, w * p
            at = y_row(f, j)
            yg[at] = g
            yh[at] = h
            yq[at] = p
            for box, item in zip(out_state, (g * w, 1.0 + h * m, first[f] + g * m)):
                box.append(item)
        return (nu_next,) + tuple(tuple(box) for box in out_state)

    nu, edge, mass, first = lax.fori_loop(1, NY - 1, forward, start)
    at = 0
    y_at = []
    for group in GROUPS:
        y_at.append(at)
        for v, values in enumerate((first, mass, edge)):
            for f in group:
                sends["ym"][share("ym", at)] = values[f]
                at += 1
    sends["ym"][share("ym", at)] = nu0
    sends["ym"][share("ym", at + 1)] = nu
    send("ym")
    keep("ym")

    for s in range(2):
        for f in range(FIELDS):
            for i, ends in ((0, (one, zero)), (NX - 1, (zero, one))):
                at = x_row(f, i, s)
                xa[at], xb[at], xp[at] = ends[0], ends[1], zero

        def backward(k, state, s=s):
            i = NX - 2 - k
            new = []
            for f in range(FIELDS):
                a, b, p = state[f]
                at = x_row(f, i, s)
                h = xh[at]
                a, b, p = xg[at] + h * a, h * b, xq[at] + h * p
                xa[at], xb[at], xp[at] = a, b, p
                new.append((a, b, p))
            return tuple(new)

        lax.fori_loop(0, NX - 2, backward, ((zero, one, zero),) * FIELDS)

    line = lax.broadcasted_iota(jnp.int32, (8, LANES), 0)

    def rates(group, each):
        value = jnp.full((8, LANES), rate[group[-1]], jnp.float32)
        for place, f in enumerate(group[:-1]):
            value = jnp.where(line // each == place, rate[f], value)
        return value

    for g, group in enumerate(GROUPS):
        what, n = ("xo", g), 2 * len(group)
        rate_x = rates(group, 2)

        def end_visc(k, v):
            base = 10 * len(GROUPS[0]) + 2 * v
            low, high = (recvs["xo", 0][peer_rows(("xo", 0), k, base + s, 1)] for s in range(2))
            return jnp.where(line % 2 == 1, high, low)

        def link(j):
            if j % 2 == 0:
                return recvs[what][peer_rows(what, j // 2, 2 * n)]
            return rate_x * (end_visc(j // 2, 1) + end_visc(j // 2 + 1, 0))

        total(what).wait_recv()
        parts = chain_matrix(
            lambda j: recvs[what][peer_rows(what, j // 2, n * (j % 2))],
            link,
            2.0 * rate_x * end_visc(0, 0),
            2.0 * rate_x * end_visc(PEERS - 1, 1),
            PEERS,
        )
        solved = chain_solve(parts, lambda j: recvs[what][peer_rows(what, j // 2, n * (3 + j % 2))], PEERS)
        back = ("xv", g)
        for k in range(PEERS):
            for v in range(2):
                sends[back][peer_rows(back, k, n * v, n)] = solved[2 * k + v][:n]
        send(back, x_order[:7])
        keep(back)
    for g in range(len(GROUPS)):
        send(("xv", g), x_order[7:])

    def natural(f, j):
        return pl.ds(f * ROWS + j, 16, stride=NY)

    for f in range(FIELDS):
        for j, ends in ((0, (one, zero)), (NY - 1, (zero, one))):
            at = natural(f, j)
            ya[at], yb[at], yp[at] = ends[0], ends[1], zero

    def backward(k, state):
        j = NY - 2 - k
        new = []
        for f in range(FIELDS):
            a, b = state[f]
            at = y_row(f, j)
            h = yh[at]
            a, b = yg[at] + h * a, h * b
            ya[natural(f, j)], yb[natural(f, j)] = a, b
            new.append((a, b))
        return tuple(new)

    lax.fori_loop(0, NY - 2, backward, ((zero, one),) * FIELDS)

    total("ym").wait_recv()
    middles = []
    for g, group in enumerate(GROUPS):
        n = len(group)
        rate_y = rates(group, 1)

        def end_visc(k, v):
            return recvs["ym"][peer_rows("ym", k, 3 * FIELDS + v, 1)]

        def link(j):
            if j % 2 == 0:
                return recvs["ym"][peer_rows("ym", j // 2, y_at[g] + 2 * n)]
            return rate_y * (end_visc(j // 2, 1) + end_visc(j // 2 + 1, 0))

        low, high, middle = chain_matrix(
            lambda j: recvs["ym"][peer_rows("ym", j // 2, y_at[g] + n * (j % 2))],
            link,
            2.0 * rate_y * end_visc(0, 0),
            2.0 * rate_y * end_visc(PEERS - 1, 1),
            PEERS,
        )
        middles.append(middle)
        for side, steps in enumerate((low, high)):
            for j, (p, h) in enumerate(steps):
                at = rows(((2 * g + side) * PEERS + j) * 8, 8)
                chain_p[at] = p
                chain_h[at] = h

    for g, group in enumerate(GROUPS):
        what, back, n = ("yr", g), ("xv", g), len(group)
        total(back).wait_recv()
        for place, f in enumerate(group):
            low_end, high_end = (
                jnp.concatenate(
                    [recvs[back][share(back, 2 * n * v + 2 * place + s)] for s in range(2)], axis=0
                )
                for v in range(2)
            )

            def finish_x(i, carry, f=f, place=place, low_end=low_end, high_end=high_end):
                at = rows(pl.multiple_of(f * ROWS + i * NY, NY), NY)
                value = xp[at] + xa[at] * low_end + xb[at] * high_end
                half[at] = value
                low = jnp.sum(ya[at] * value, axis=0, keepdims=True)
                high = jnp.sum(yb[at] * value, axis=0, keepdims=True)
                sends[what][peer_rows(what, i, place, 1)] = low
                sends[what][peer_rows(what, i, n + place, 1)] = high
                return carry

            lax.fori_loop(0, NX, finish_x, 0, unroll=8)
        send(what)
        keep(what)

    def forward(j, right):
        new = []
        for f in range(FIELDS):
            at = y_row(f, j)
            yg[at] = yq[at] * right[f]
            new.append(half[natural(f, j + 1)] + yh[at] * right[f])
        return tuple(new)

    lax.fori_loop(1, NY - 1, forward, tuple(half[natural(f, 1)] for f in range(FIELDS)))

    def backward(k, state):
        j = NY - 2 - k
        new = []
        for f in range(FIELDS):
            at = y_row(f, j)
            p = yg[at] + yh[at] * state[f]
            yp[natural(f, j)] = p
            new.append(p)
        return tuple(new)

    lax.fori_loop(0, NY - 2, backward, (zero,) * FIELDS)

    for g, group in enumerate(GROUPS):
        what, back, n = ("yr", g), ("yv", g), len(group)
        parts = []
        for side in range(2):
            at = [rows(((2 * g + side) * PEERS + j) * 8, 8) for j in range(PEERS - 1)]
            parts.append([(chain_p[place], chain_h[place]) for place in at])
        total(what).wait_recv()
        solved = chain_solve(
            (*parts, middles[g]), lambda j: recvs[what][peer_rows(what, j // 2, n * (j % 2))], PEERS
        )
        for k in range(PEERS):
            for v in range(2):
                sends[back][peer_rows(back, k, n * v, n)] = solved[2 * k + v][:n]
        send(back, y_order)
        keep(back)

    for g, group in enumerate(GROUPS):
        back, n = ("yv", g), len(group)
        total(back).wait_recv()

        def finish_y(i, carry):
            for place, f in enumerate(group):
                at = rows(pl.multiple_of(f * ROWS + i * NY, NY), NY)
                low_end = recvs[back][peer_rows(back, i, place, 1)]
                high_end = recvs[back][peer_rows(back, i, n + place, 1)]
                out[at] = yp[at] + ya[at] * low_end + yb[at] * high_end
            return carry

        lax.fori_loop(0, NX, finish_y, 0, unroll=2)
    for what in MESSAGES:
        total(what).wait_send()


def shards(conserved_states, thermal_level, spread_factors):
    def buffer(count):
        return pltpu.VMEM((count, LANES), jnp.float32)

    whole = buffer(FIELDS * ROWS)
    messages = [buffer(PEERS * size) for axis, count, size in MESSAGES.values()]
    arrivals = [buffer(PEERS * size + 8) for axis, count, size in MESSAGES.values()]
    solved = pl.pallas_call(
        kernel,
        out_shape=pltpu.VMEM((FIELDS * ROWS, LANES), jnp.float32),
        in_specs=[
            pl.BlockSpec(memory_space=pl.ANY),
            pl.BlockSpec(memory_space=pl.ANY),
            pl.BlockSpec(memory_space=pltpu.SMEM),
        ],
        out_specs=pl.BlockSpec(memory_space=pltpu.VMEM),
        scratch_shapes=[whole, buffer(ROWS), buffer(ROWS)]
        + [whole] * 13
        + messages
        + arrivals
        + [
            buffer(2 * len(GROUPS) * PEERS * 8),
            buffer(2 * len(GROUPS) * PEERS * 8),
            pltpu.SemaphoreType.DMA((len(MESSAGES),)),
            pltpu.SemaphoreType.DMA((len(MESSAGES),)),
            pltpu.SemaphoreType.DMA((2,)),
        ],
        compiler_params=pltpu.CompilerParams(
            collective_id=0, has_side_effects=True, vmem_limit_bytes=60 * 1024 * 1024
        ),
    )(
        conserved_states.reshape(FIELDS * ROWS, LANES),
        thermal_level.reshape(ROWS, LANES),
        spread_factors,
    )
    return solved.reshape(conserved_states.shape)


def solution(mesh):
    return jax.shard_map(
        shards,
        mesh=mesh,
        in_specs=(P(None, "gx", "gy", None), P("gx", "gy", None), P()),
        out_specs=P(None, "gx", "gy", None),
        check_vma=False,
    )
```

```python
import jax
import jax.numpy as jnp
from jax import lax
from jax.experimental import pallas as pl
from jax.experimental.pallas import tpu as pltpu
from jax.sharding import PartitionSpec as P

MESH = pl.DeviceIdType.MESH
FIELDS, NX, NY, LANES = 5, 16, 32, 128
PEERS = 16
ROWS = NX * NY
GROUPS = ((0, 1, 2), (3, 4))


def message_table():
    table = {"ym": ("gy", 3 * FIELDS + 2, 24)}
    for g, group in enumerate(GROUPS):
        n = len(group)
        for name, axis, count in (
            ("xo", "gx", 10 * n + (4 if g == 0 else 0)),
            ("xv", "gx", 4 * n),
            ("yr", "gy", 2 * n),
            ("yv", "gy", 2 * n),
        ):
            table[name, g] = (axis, count, -(-count // 8) * 8)
    return table


MESSAGES = message_table()
ORDER = {what: k for k, what in enumerate(MESSAGES)}

X_STEPS = (
    (2, 2), (2, 1), (1, 2), (2, 3), (3, 2), (1, 1), (1, 3), (3, 1),
    (3, 3), (0, 2), (2, 0), (0, 1), (1, 0), (0, 3), (3, 0),
)
Y_STEPS = (
    (4, 0), (4, 1), (3, 0), (3, 1), (5, 0), (5, 1), (2, 0), (2, 1),
    (6, 0), (6, 1), (1, 0), (1, 1), (7, 0), (7, 1), (0, 1),
)


X_FIRST = tuple(range(16))
Y_FIRST = (1, 3, 9, 5, 8, 2, 7, 11, 4, 10, 6, 13, 15, 12, 0, 14)


def ring(step, size):
    return min(step, size - step)


def others(order, me):
    place = sum(k * (me == at).astype(jnp.int32) for k, at in enumerate(order))
    return [jnp.where(place > k, order[k], order[k + 1]) for k in range(len(order) - 1)]


def partners(axis, gx, gy):
    if axis == "gx":
        return [(((gx + 4 * i) & 12) + ((gx + j) & 3), gy) for i, j in X_STEPS]
    return [(gx, ((gy + 2 * i) & 14) + ((gy + j) & 1)) for i, j in Y_STEPS]


def rows(start, count):
    return pl.ds(start, count)


def chain_matrix(mass, link, wall_low, wall_high, count):
    masses = [mass(j) for j in range(count)]
    links = [link(j) for j in range(count - 1)]
    masses[0] += wall_low
    masses[-1] += wall_high
    nodes, steps = list(range(count)), []
    while len(nodes) > 1:
        fewer = []
        for at in range(1, len(nodes), 2):
            low, j = nodes[at - 1], nodes[at]
            high = nodes[at + 1] if at + 1 < len(nodes) else None
            m, a = masses[j], links[at - 1]
            b = links[at] if high is not None else None
            p = 1.0 / (m + a if high is None else m + (a + b))
            g = a * p
            h = None if high is None else b * p
            steps.append((low, j, high, p, g, h))
            masses[low] += g * m
            if high is not None:
                masses[high] += h * m
                fewer.append(g * b)
        nodes, links = nodes[::2], fewer
    return steps, 1.0 / masses[0]


def chain_solve(steps, last, right, count):
    values = [right(j) for j in range(count)]
    kept = []
    for low, j, high, p, g, h in steps:
        r = values[j]
        kept.append(p * r)
        values[low] += g * r
        if high is not None:
            values[high] += h * r
    values[0] = last * values[0]
    for (low, j, high, p, g, h), q in zip(reversed(steps), reversed(kept)):
        q = q + g * values[low]
        values[j] = q if high is None else q + h * values[high]
    return values


def kernel(
    fields_hbm, level_hbm, spread_hbm, out,
    spread, field, level, visc, xg, xh, xq, xa, xb, xp, half, yg, yh, yq, ya, yb, yp,
    *rest,
):
    gx, gy = lax.axis_index("gx"), lax.axis_index("gy")
    count = len(MESSAGES)
    sends = dict(zip(MESSAGES, rest[:count]))
    recvs = dict(zip(MESSAGES, rest[count : 2 * count]))
    chain_p, chain_g, chain_h, send_sem, recv_sem, in_sem = rest[2 * count :]
    everyone = partners("gx", gx, gy) + partners("gy", gx, gy)
    hops = [ring(i, 4) + ring(j, 4) for i, j in X_STEPS] + [ring(i, 8) for i, j in Y_STEPS]
    greeted = [everyone[k] for k in sorted(range(len(everyone)), key=lambda k: -hops[k])]

    barrier = pltpu.get_barrier_semaphore()
    for device in greeted:
        pl.semaphore_signal(barrier, inc=1, device_id=device, device_id_type=MESH)
    level_in = pltpu.make_async_copy(level_hbm, level, in_sem.at[0])
    fields_in = pltpu.make_async_copy(fields_hbm, field, in_sem.at[1])
    spread_in = pltpu.make_async_copy(spread_hbm, spread, in_sem.at[2])
    level_in.start()
    spread_in.start()
    fields_in.start()

    x_order = [(peer, gy) for peer in others(X_FIRST, gx)]
    y_order = [(gx, peer) for peer in others(Y_FIRST, gy)]

    def send(what, devices=None):
        axis, count, size = MESSAGES[what]
        me = gx if axis == "gx" else gy
        for device in devices or partners(axis, gx, gy):
            peer = device[0] if axis == "gx" else device[1]
            pltpu.make_async_remote_copy(
                src_ref=sends[what].at[rows(pl.multiple_of(peer * size, 8), count)],
                dst_ref=recvs[what].at[rows(pl.multiple_of(me * size, 8), count)],
                send_sem=send_sem.at[ORDER[what]],
                recv_sem=recv_sem.at[ORDER[what]],
                device_id=device,
                device_id_type=MESH,
            ).start()

    def keep(what):
        axis, count, size = MESSAGES[what]
        mine = rows(pl.multiple_of((gx if axis == "gx" else gy) * size, 8), size)
        recvs[what][mine] = sends[what][mine]

    def total(what):
        axis, count, size = MESSAGES[what]
        part = rows(0, (PEERS - 1) * count)
        return pltpu.make_async_remote_copy(
            src_ref=sends[what].at[part],
            dst_ref=recvs[what].at[part],
            send_sem=send_sem.at[ORDER[what]],
            recv_sem=recv_sem.at[ORDER[what]],
            device_id=everyone[0],
            device_id_type=MESH,
        )

    def share(what, row):
        return pl.ds(row, PEERS, stride=MESSAGES[what][2])

    def peer_rows(what, k, row, count=8):
        return rows(k * MESSAGES[what][2] + row, count)

    spread_in.wait()
    rate = [2500.0 * spread[f] for f in range(FIELDS)]
    zero = jnp.zeros((16, LANES), jnp.float32)
    one = jnp.ones((16, LANES), jnp.float32)

    for what, (axis, used, size) in MESSAGES.items():
        for row in range(used, size):
            sends[what][share(what, row)] = zero
            recvs[what][share(what, row)] = zero
        recvs[what][rows(PEERS * size, 8)] = zero[:8]

    level_in.wait()

    def power(t, carry):
        at = rows(pl.multiple_of(t * 64, 64), 64)
        visc[at] = jnp.exp(0.7 * jnp.log(level[at]))
        return carry

    lax.fori_loop(0, ROWS // 64, power, 0)
    fields_in.wait()

    def x_row(f, i, s):
        return rows(pl.multiple_of(f * ROWS + i * NY + s * 16, 16), 16)

    def x_visc(i, s):
        return visc[rows(pl.multiple_of(i * NY + s * 16, 16), 16)]

    for s in range(2):
        nu0, nu1 = x_visc(0, s), x_visc(1, s)
        start = (
            nu1,
            tuple(rate[f] * (nu0 + nu1) for f in range(FIELDS)),
            (one,) * FIELDS,
            (one,) * FIELDS,
            tuple(field[x_row(f, 1, s)] for f in range(FIELDS)),
            tuple(field[x_row(f, 0, s)] for f in range(FIELDS)),
        )

        def forward(i, state, s=s):
            nu, edge, mass, first, right, first_right = state
            nu_next = x_visc(i + 1, s)
            face = nu + nu_next
            out_state = ([], [], [], [], [])
            for f in range(FIELDS):
                e, m, r = edge[f], mass[f], right[f]
                w = rate[f] * face
                p = 1.0 / (e + w + m)
                g, h = e * p, w * p
                at = x_row(f, i, s)
                xg[at] = g
                xh[at] = h
                xq[at] = p * r
                for box, item in zip(
                    out_state,
                    (g * w, 1.0 + h * m, first[f] + g * m, field[x_row(f, i + 1, s)] + h * r, first_right[f] + g * r),
                ):
                    box.append(item)
            return (nu_next,) + tuple(tuple(box) for box in out_state)

        nu, edge, mass, first, right, first_right = lax.fori_loop(1, NX - 1, forward, start)
        for g, group in enumerate(GROUPS):
            what, n = ("xo", g), 2 * len(group)
            for place, f in enumerate(group):
                for v, value in enumerate((first[f], mass[f], edge[f], first_right[f], right[f])):
                    sends[what][share(what, v * n + 2 * place + s)] = value
        what, n = ("xo", 0), 10 * len(GROUPS[0])
        sends[what][share(what, n + s)] = nu0
        sends[what][share(what, n + 2 + s)] = nu

    pl.semaphore_wait(barrier, len(everyone))
    for g in range(len(GROUPS)):
        send(("xo", g))
    for g in range(len(GROUPS)):
        keep(("xo", g))

    def y_visc(j):
        return visc[pl.ds(j, 16, stride=NY)]

    def y_row(f, j):
        return rows(pl.multiple_of((f * NY + j) * 16, 16), 16)

    nu0, nu1 = y_visc(0), y_visc(1)
    start = (nu1, tuple(rate[f] * (nu0 + nu1) for f in range(FIELDS)), (one,) * FIELDS, (one,) * FIELDS)

    def forward(j, state):
        nu, edge, mass, first = state
        nu_next = y_visc(j + 1)
        face = nu + nu_next
        out_state = ([], [], [])
        for f in range(FIELDS):
            e, m = edge[f], mass[f]
            w = rate[f] * face
            p = 1.0 / (e + w + m)
            g, h = e * p, w * p
            at = y_row(f, j)
            yg[at] = g
            yh[at] = h
            yq[at] = p
            for box, item in zip(out_state, (g * w, 1.0 + h * m, first[f] + g * m)):
                box.append(item)
        return (nu_next,) + tuple(tuple(box) for box in out_state)

    nu, edge, mass, first = lax.fori_loop(1, NY - 1, forward, start)
    at = 0
    y_at = []
    for group in GROUPS:
        y_at.append(at)
        for v, values in enumerate((first, mass, edge)):
            for f in group:
                sends["ym"][share("ym", at)] = values[f]
                at += 1
    sends["ym"][share("ym", at)] = nu0
    sends["ym"][share("ym", at + 1)] = nu
    send("ym")
    keep("ym")

    for s in range(2):
        for f in range(FIELDS):
            for i, ends in ((0, (one, zero)), (NX - 1, (zero, one))):
                at = x_row(f, i, s)
                xa[at], xb[at], xp[at] = ends[0], ends[1], zero

        def backward(k, state, s=s):
            i = NX - 2 - k
            new = []
            for f in range(FIELDS):
                a, b, p = state[f]
                at = x_row(f, i, s)
                h = xh[at]
                a, b, p = xg[at] + h * a, h * b, xq[at] + h * p
                xa[at], xb[at], xp[at] = a, b, p
                new.append((a, b, p))
            return tuple(new)

        lax.fori_loop(0, NX - 2, backward, ((zero, one, zero),) * FIELDS)

    line = lax.broadcasted_iota(jnp.int32, (8, LANES), 0)

    def rates(group, each):
        value = jnp.full((8, LANES), rate[group[-1]], jnp.float32)
        for place, f in enumerate(group[:-1]):
            value = jnp.where(line // each == place, rate[f], value)
        return value

    for g, group in enumerate(GROUPS):
        what, n = ("xo", g), 2 * len(group)
        rate_x = rates(group, 2)

        def end_visc(k, v):
            base = 10 * len(GROUPS[0]) + 2 * v
            low, high = (recvs["xo", 0][peer_rows(("xo", 0), k, base + s, 1)] for s in range(2))
            return jnp.where(line % 2 == 1, high, low)

        def link(j):
            if j % 2 == 0:
                return recvs[what][peer_rows(what, j // 2, 2 * n)]
            return rate_x * (end_visc(j // 2, 1) + end_visc(j // 2 + 1, 0))

        total(what).wait_recv()
        steps, last = chain_matrix(
            lambda j: recvs[what][peer_rows(what, j // 2, n * (j % 2))],
            link,
            2.0 * rate_x * end_visc(0, 0),
            2.0 * rate_x * end_visc(PEERS - 1, 1),
            2 * PEERS,
        )
        solved = chain_solve(
            steps, last, lambda j: recvs[what][peer_rows(what, j // 2, n * (3 + j % 2))], 2 * PEERS
        )
        back = ("xv", g)
        for k in range(PEERS):
            for v in range(2):
                sends[back][peer_rows(back, k, n * v, n)] = solved[2 * k + v][:n]
        send(back, x_order[:7])
        keep(back)
    for g in range(len(GROUPS)):
        send(("xv", g), x_order[7:])

    def natural(f, j):
        return pl.ds(f * ROWS + j, 16, stride=NY)

    for f in range(FIELDS):
        for j, ends in ((0, (one, zero)), (NY - 1, (zero, one))):
            at = natural(f, j)
            ya[at], yb[at], yp[at] = ends[0], ends[1], zero

    def backward(k, state):
        j = NY - 2 - k
        new = []
        for f in range(FIELDS):
            a, b = state[f]
            at = y_row(f, j)
            h = yh[at]
            a, b = yg[at] + h * a, h * b
            ya[natural(f, j)], yb[natural(f, j)] = a, b
            new.append((a, b))
        return tuple(new)

    lax.fori_loop(0, NY - 2, backward, ((zero, one),) * FIELDS)

    total("ym").wait_recv()
    y_steps, y_last = [], []
    for g, group in enumerate(GROUPS):
        n = len(group)
        rate_y = rates(group, 1)

        def end_visc(k, v):
            return recvs["ym"][peer_rows("ym", k, 3 * FIELDS + v, 1)]

        def link(j):
            if j % 2 == 0:
                return recvs["ym"][peer_rows("ym", j // 2, y_at[g] + 2 * n)]
            return rate_y * (end_visc(j // 2, 1) + end_visc(j // 2 + 1, 0))

        steps, last = chain_matrix(
            lambda j: recvs["ym"][peer_rows("ym", j // 2, y_at[g] + n * (j % 2))],
            link,
            2.0 * rate_y * end_visc(0, 0),
            2.0 * rate_y * end_visc(PEERS - 1, 1),
            2 * PEERS,
        )
        y_last.append(last)
        y_steps.append([(low, j, high) for low, j, high, *values in steps])
        for low, j, high, *values in steps:
            for kept, value in zip((chain_p, chain_g, chain_h), values):
                if value is not None:
                    kept[rows((2 * g * PEERS + j) * 8, 8)] = value

    for g, group in enumerate(GROUPS):
        what, back, n = ("yr", g), ("xv", g), len(group)
        total(back).wait_recv()
        for place, f in enumerate(group):
            low_end, high_end = (
                jnp.concatenate(
                    [recvs[back][share(back, 2 * n * v + 2 * place + s)] for s in range(2)], axis=0
                )
                for v in range(2)
            )

            def finish_x(i, carry, f=f, place=place, low_end=low_end, high_end=high_end):
                at = rows(pl.multiple_of(f * ROWS + i * NY, NY), NY)
                value = xp[at] + xa[at] * low_end + xb[at] * high_end
                half[at] = value
                low = jnp.sum(ya[at] * value, axis=0, keepdims=True)
                high = jnp.sum(yb[at] * value, axis=0, keepdims=True)
                sends[what][peer_rows(what, i, place, 1)] = low
                sends[what][peer_rows(what, i, n + place, 1)] = high
                return carry

            lax.fori_loop(0, NX, finish_x, 0, unroll=16)
        send(what)
        keep(what)

    def forward(j, right):
        new = []
        for f in range(FIELDS):
            at = y_row(f, j)
            yg[at] = yq[at] * right[f]
            new.append(half[natural(f, j + 1)] + yh[at] * right[f])
        return tuple(new)

    lax.fori_loop(1, NY - 1, forward, tuple(half[natural(f, 1)] for f in range(FIELDS)))

    def backward(k, state):
        j = NY - 2 - k
        new = []
        for f in range(FIELDS):
            at = y_row(f, j)
            p = yg[at] + yh[at] * state[f]
            yp[natural(f, j)] = p
            new.append(p)
        return tuple(new)

    lax.fori_loop(0, NY - 2, backward, (zero,) * FIELDS)

    for g, group in enumerate(GROUPS):
        what, back, n = ("yr", g), ("yv", g), len(group)
        total(what).wait_recv()
        steps = [
            (low, j, high, *(kept[rows((2 * g * PEERS + j) * 8, 8)] for kept in (chain_p, chain_g, chain_h)))
            for low, j, high in y_steps[g]
        ]
        solved = chain_solve(
            steps, y_last[g], lambda j: recvs[what][peer_rows(what, j // 2, n * (j % 2))], 2 * PEERS
        )
        for k in range(PEERS):
            for v in range(2):
                sends[back][peer_rows(back, k, n * v, n)] = solved[2 * k + v][:n]
        send(back, y_order)
        keep(back)

    for g, group in enumerate(GROUPS):
        back, n = ("yv", g), len(group)
        total(back).wait_recv()

        def finish_y(i, carry):
            for place, f in enumerate(group):
                at = rows(pl.multiple_of(f * ROWS + i * NY, NY), NY)
                low_end = recvs[back][peer_rows(back, i, place, 1)]
                high_end = recvs[back][peer_rows(back, i, n + place, 1)]
                out[at] = yp[at] + ya[at] * low_end + yb[at] * high_end
            return carry

        lax.fori_loop(0, NX, finish_y, 0, unroll=4)
    for what in MESSAGES:
        total(what).wait_send()


def shards(conserved_states, thermal_level, spread_factors):
    def buffer(count):
        return pltpu.VMEM((count, LANES), jnp.float32)

    whole = buffer(FIELDS * ROWS)
    messages = [buffer(PEERS * size) for axis, count, size in MESSAGES.values()]
    arrivals = [buffer(PEERS * size + 8) for axis, count, size in MESSAGES.values()]
    solved = pl.pallas_call(
        kernel,
        out_shape=pltpu.VMEM((FIELDS * ROWS, LANES), jnp.float32),
        in_specs=[
            pl.BlockSpec(memory_space=pl.ANY),
            pl.BlockSpec(memory_space=pl.ANY),
            pl.BlockSpec(memory_space=pl.ANY),
        ],
        out_specs=pl.BlockSpec(memory_space=pltpu.VMEM),
        scratch_shapes=[pltpu.SMEM((FIELDS,), jnp.float32), whole, buffer(ROWS), buffer(ROWS)]
        + [whole] * 13
        + messages
        + arrivals
        + [
            buffer(2 * len(GROUPS) * PEERS * 8),
            buffer(2 * len(GROUPS) * PEERS * 8),
            buffer(2 * len(GROUPS) * PEERS * 8),
            pltpu.SemaphoreType.DMA((len(MESSAGES),)),
            pltpu.SemaphoreType.DMA((len(MESSAGES),)),
            pltpu.SemaphoreType.DMA((3,)),
        ],
        compiler_params=pltpu.CompilerParams(
            collective_id=0, has_side_effects=True, vmem_limit_bytes=60 * 1024 * 1024
        ),
    )(
        conserved_states.reshape(FIELDS * ROWS, LANES),
        thermal_level.reshape(ROWS, LANES),
        spread_factors,
    )
    return solved.reshape(conserved_states.shape)


def solution(mesh):
    return jax.shard_map(
        shards,
        mesh=mesh,
        in_specs=(P(None, "gx", "gy", None), P("gx", "gy", None), P()),
        out_specs=P(None, "gx", "gy", None),
        check_vma=False,
    )
```

```python
import jax
import jax.numpy as jnp
from jax import lax
from jax.experimental import pallas as pl
from jax.experimental.pallas import tpu as pltpu
from jax.sharding import PartitionSpec as P

MESH = pl.DeviceIdType.MESH
FIELDS, NX, NY, LANES = 5, 16, 32, 128
PEERS = 16
ROWS = NX * NY
GROUPS = ((0, 1, 2), (3, 4))


def message_table():
    table = {"ym": ("gy", 3 * FIELDS + 2, 24)}
    for g, group in enumerate(GROUPS):
        n = len(group)
        for name, axis, count in (
            ("xo", "gx", 10 * n + (4 if g == 0 else 0)),
            ("xv", "gx", 4 * n),
            ("yr", "gy", 2 * n),
            ("yv", "gy", 2 * n),
        ):
            table[name, g] = (axis, count, -(-count // 8) * 8)
    return table


MESSAGES = message_table()
ORDER = {what: k for k, what in enumerate(MESSAGES)}

X_STEPS = (
    (2, 2), (2, 1), (1, 2), (2, 3), (3, 2), (1, 1), (1, 3), (3, 1),
    (3, 3), (0, 2), (2, 0), (0, 1), (1, 0), (0, 3), (3, 0),
)
Y_STEPS = (
    (4, 0), (4, 1), (3, 0), (3, 1), (5, 0), (5, 1), (2, 0), (2, 1),
    (6, 0), (6, 1), (1, 0), (1, 1), (7, 0), (7, 1), (0, 1),
)


X_FIRST = tuple(range(16))
Y_FIRST = (1, 3, 9, 5, 8, 2, 7, 11, 4, 10, 6, 13, 15, 12, 0, 14)


def ring(step, size):
    return min(step, size - step)


def others(order, me):
    place = sum(k * (me == at).astype(jnp.int32) for k, at in enumerate(order))
    return [jnp.where(place > k, order[k], order[k + 1]) for k in range(len(order) - 1)]


def partners(axis, gx, gy):
    if axis == "gx":
        return [(((gx + 4 * i) & 12) + ((gx + j) & 3), gy) for i, j in X_STEPS]
    return [(gx, ((gy + 2 * i) & 14) + ((gy + j) & 1)) for i, j in Y_STEPS]


def rows(start, count):
    return pl.ds(start, count)


def chain_matrix(mass, link, wall_low, wall_high, count):
    masses = [mass(j) for j in range(count)]
    links = [link(j) for j in range(count - 1)]
    masses[0] += wall_low
    masses[-1] += wall_high
    nodes, steps = list(range(count)), []
    while len(nodes) > 1:
        fewer = []
        for at in range(1, len(nodes), 2):
            low, j = nodes[at - 1], nodes[at]
            high = nodes[at + 1] if at + 1 < len(nodes) else None
            m, a = masses[j], links[at - 1]
            b = links[at] if high is not None else None
            p = 1.0 / (m + a if high is None else m + (a + b))
            g = a * p
            h = None if high is None else b * p
            steps.append((low, j, high, p, g, h))
            masses[low] += g * m
            if high is not None:
                masses[high] += h * m
                fewer.append(g * b)
        nodes, links = nodes[::2], fewer
    return steps, 1.0 / masses[0]


def chain_solve(steps, last, right, count):
    values = [right(j) for j in range(count)]
    kept = []
    for low, j, high, p, g, h in steps:
        r = values[j]
        kept.append(p * r)
        values[low] += g * r
        if high is not None:
            values[high] += h * r
    values[0] = last * values[0]
    for (low, j, high, p, g, h), q in zip(reversed(steps), reversed(kept)):
        q = q + g * values[low]
        values[j] = q if high is None else q + h * values[high]
    return values


def kernel(
    fields_hbm, level_hbm, spread_hbm, out,
    spread, field, level, visc, xg, xh, xq, xa, xb, xp, half, yg, yh, yq, ya, yb, yp,
    *rest,
):
    gx, gy = lax.axis_index("gx"), lax.axis_index("gy")
    count = len(MESSAGES)
    sends = dict(zip(MESSAGES, rest[:count]))
    recvs = dict(zip(MESSAGES, rest[count : 2 * count]))
    chain_p, chain_g, chain_h, send_sem, recv_sem, in_sem, line_sem, all_sem = rest[2 * count :]
    everyone = partners("gx", gx, gy) + partners("gy", gx, gy)

    front = gx < 4
    my_line = [(((gx + 4 * i) & 12) + (gx & 3), gy) for i in (2, 1, 3)]
    x_partners, y_partners = partners("gx", gx, gy), partners("gy", gx, gy)

    def tell(sem, devices):
        for device in devices:
            pl.semaphore_signal(sem, inc=1, device_id=device, device_id_type=MESH)

    barrier = pltpu.get_barrier_semaphore()
    tell(barrier, x_partners)

    @pl.when(front)
    def _():
        tell(barrier, y_partners)

    level_in = pltpu.make_async_copy(level_hbm, level, in_sem.at[0])
    fields_in = pltpu.make_async_copy(fields_hbm, field, in_sem.at[1])
    spread_in = pltpu.make_async_copy(spread_hbm, spread, in_sem.at[2])
    level_in.start()
    spread_in.start()
    fields_in.start()

    x_order = [(peer, gy) for peer in others(X_FIRST, gx)]
    y_order = [(gx, peer) for peer in others(Y_FIRST, gy)]

    def send(what, devices=None):
        axis, count, size = MESSAGES[what]
        me = gx if axis == "gx" else gy
        for device in devices or partners(axis, gx, gy):
            peer = device[0] if axis == "gx" else device[1]
            pltpu.make_async_remote_copy(
                src_ref=sends[what].at[rows(pl.multiple_of(peer * size, 8), count)],
                dst_ref=recvs[what].at[rows(pl.multiple_of(me * size, 8), count)],
                send_sem=send_sem.at[ORDER[what]],
                recv_sem=recv_sem.at[ORDER[what]],
                device_id=device,
                device_id_type=MESH,
            ).start()

    def keep(what):
        axis, count, size = MESSAGES[what]
        mine = rows(pl.multiple_of((gx if axis == "gx" else gy) * size, 8), size)
        recvs[what][mine] = sends[what][mine]

    def total(what):
        axis, count, size = MESSAGES[what]
        part = rows(0, (PEERS - 1) * count)
        return pltpu.make_async_remote_copy(
            src_ref=sends[what].at[part],
            dst_ref=recvs[what].at[part],
            send_sem=send_sem.at[ORDER[what]],
            recv_sem=recv_sem.at[ORDER[what]],
            device_id=everyone[0],
            device_id_type=MESH,
        )

    def share(what, row):
        return pl.ds(row, PEERS, stride=MESSAGES[what][2])

    def peer_rows(what, k, row, count=8):
        return rows(k * MESSAGES[what][2] + row, count)

    spread_in.wait()
    rate = [2500.0 * spread[f] for f in range(FIELDS)]
    zero = jnp.zeros((16, LANES), jnp.float32)
    one = jnp.ones((16, LANES), jnp.float32)

    for what, (axis, used, size) in MESSAGES.items():
        for row in range(used, size):
            sends[what][share(what, row)] = zero
            recvs[what][share(what, row)] = zero
        recvs[what][rows(PEERS * size, 8)] = zero[:8]

    level_in.wait()

    def power(t, carry):
        at = rows(pl.multiple_of(t * 64, 64), 64)
        visc[at] = jnp.exp(0.7 * jnp.log(level[at]))
        return carry

    lax.fori_loop(0, ROWS // 64, power, 0)
    fields_in.wait()

    def x_row(f, i, s):
        return rows(pl.multiple_of(f * ROWS + i * NY + s * 16, 16), 16)

    def x_visc(i, s):
        return visc[rows(pl.multiple_of(i * NY + s * 16, 16), 16)]

    for s in range(2):
        nu0, nu1 = x_visc(0, s), x_visc(1, s)
        start = (
            nu1,
            tuple(rate[f] * (nu0 + nu1) for f in range(FIELDS)),
            (one,) * FIELDS,
            (one,) * FIELDS,
            tuple(field[x_row(f, 1, s)] for f in range(FIELDS)),
            tuple(field[x_row(f, 0, s)] for f in range(FIELDS)),
        )

        def forward(i, state, s=s):
            nu, edge, mass, first, right, first_right = state
            nu_next = x_visc(i + 1, s)
            face = nu + nu_next
            out_state = ([], [], [], [], [])
            for f in range(FIELDS):
                e, m, r = edge[f], mass[f], right[f]
                w = rate[f] * face
                p = 1.0 / (e + w + m)
                g, h = e * p, w * p
                at = x_row(f, i, s)
                xg[at] = g
                xh[at] = h
                xq[at] = p * r
                for box, item in zip(
                    out_state,
                    (g * w, 1.0 + h * m, first[f] + g * m, field[x_row(f, i + 1, s)] + h * r, first_right[f] + g * r),
                ):
                    box.append(item)
            return (nu_next,) + tuple(tuple(box) for box in out_state)

        nu, edge, mass, first, right, first_right = lax.fori_loop(1, NX - 1, forward, start)
        for g, group in enumerate(GROUPS):
            what, n = ("xo", g), 2 * len(group)
            for place, f in enumerate(group):
                for v, value in enumerate((first[f], mass[f], edge[f], first_right[f], right[f])):
                    sends[what][share(what, v * n + 2 * place + s)] = value
        what, n = ("xo", 0), 10 * len(GROUPS[0])
        sends[what][share(what, n + s)] = nu0
        sends[what][share(what, n + 2 + s)] = nu

    pl.semaphore_wait(barrier, jnp.where(front, len(everyone), len(x_partners)))
    for g in range(len(GROUPS)):
        send(("xo", g))

    @pl.when(front)
    def _():
        tell(line_sem, y_partners)

    for g in range(len(GROUPS)):
        keep(("xo", g))

    def y_visc(j):
        return visc[pl.ds(j, 16, stride=NY)]

    def y_row(f, j):
        return rows(pl.multiple_of((f * NY + j) * 16, 16), 16)

    nu0, nu1 = y_visc(0), y_visc(1)
    start = (nu1, tuple(rate[f] * (nu0 + nu1) for f in range(FIELDS)), (one,) * FIELDS, (one,) * FIELDS)

    def forward(j, state):
        nu, edge, mass, first = state
        nu_next = y_visc(j + 1)
        face = nu + nu_next
        out_state = ([], [], [])
        for f in range(FIELDS):
            e, m = edge[f], mass[f]
            w = rate[f] * face
            p = 1.0 / (e + w + m)
            g, h = e * p, w * p
            at = y_row(f, j)
            yg[at] = g
            yh[at] = h
            yq[at] = p
            for box, item in zip(out_state, (g * w, 1.0 + h * m, first[f] + g * m)):
                box.append(item)
        return (nu_next,) + tuple(tuple(box) for box in out_state)

    nu, edge, mass, first = lax.fori_loop(1, NY - 1, forward, start)
    at = 0
    y_at = []
    for group in GROUPS:
        y_at.append(at)
        for v, values in enumerate((first, mass, edge)):
            for f in group:
                sends["ym"][share("ym", at)] = values[f]
                at += 1
    sends["ym"][share("ym", at)] = nu0
    sends["ym"][share("ym", at + 1)] = nu
    keep("ym")

    for s in range(2):
        for f in range(FIELDS):
            for i, ends in ((0, (one, zero)), (NX - 1, (zero, one))):
                at = x_row(f, i, s)
                xa[at], xb[at], xp[at] = ends[0], ends[1], zero

        def backward(k, state, s=s):
            i = NX - 2 - k
            new = []
            for f in range(FIELDS):
                a, b, p = state[f]
                at = x_row(f, i, s)
                h = xh[at]
                a, b, p = xg[at] + h * a, h * b, xq[at] + h * p
                xa[at], xb[at], xp[at] = a, b, p
                new.append((a, b, p))
            return tuple(new)

        lax.fori_loop(0, NX - 2, backward, ((zero, one, zero),) * FIELDS)

    @pl.when(front)
    def _():
        pl.semaphore_wait(line_sem, len(y_partners))
        tell(all_sem, my_line)

    line = lax.broadcasted_iota(jnp.int32, (8, LANES), 0)

    def rates(group, each):
        value = jnp.full((8, LANES), rate[group[-1]], jnp.float32)
        for place, f in enumerate(group[:-1]):
            value = jnp.where(line // each == place, rate[f], value)
        return value

    for g, group in enumerate(GROUPS):
        what, n = ("xo", g), 2 * len(group)
        rate_x = rates(group, 2)

        def end_visc(k, v):
            base = 10 * len(GROUPS[0]) + 2 * v
            low, high = (recvs["xo", 0][peer_rows(("xo", 0), k, base + s, 1)] for s in range(2))
            return jnp.where(line % 2 == 1, high, low)

        def link(j):
            if j % 2 == 0:
                return recvs[what][peer_rows(what, j // 2, 2 * n)]
            return rate_x * (end_visc(j // 2, 1) + end_visc(j // 2 + 1, 0))

        total(what).wait_recv()
        steps, last = chain_matrix(
            lambda j: recvs[what][peer_rows(what, j // 2, n * (j % 2))],
            link,
            2.0 * rate_x * end_visc(0, 0),
            2.0 * rate_x * end_visc(PEERS - 1, 1),
            2 * PEERS,
        )
        solved = chain_solve(
            steps, last, lambda j: recvs[what][peer_rows(what, j // 2, n * (3 + j % 2))], 2 * PEERS
        )
        back = ("xv", g)
        for k in range(PEERS):
            for v in range(2):
                sends[back][peer_rows(back, k, n * v, n)] = solved[2 * k + v][:n]
        send(back, x_order[:7])
        keep(back)
    for g in range(len(GROUPS)):
        send(("xv", g), x_order[7:])

    @pl.when(jnp.logical_not(front))
    def _():
        pl.semaphore_wait(all_sem, 1)

    send("ym")

    def natural(f, j):
        return pl.ds(f * ROWS + j, 16, stride=NY)

    for f in range(FIELDS):
        for j, ends in ((0, (one, zero)), (NY - 1, (zero, one))):
            at = natural(f, j)
            ya[at], yb[at], yp[at] = ends[0], ends[1], zero

    def backward(k, state):
        j = NY - 2 - k
        new = []
        for f in range(FIELDS):
            a, b = state[f]
            at = y_row(f, j)
            h = yh[at]
            a, b = yg[at] + h * a, h * b
            ya[natural(f, j)], yb[natural(f, j)] = a, b
            new.append((a, b))
        return tuple(new)

    lax.fori_loop(0, NY - 2, backward, ((zero, one),) * FIELDS)

    for g, group in enumerate(GROUPS):
        what, back, n = ("yr", g), ("xv", g), len(group)
        total(back).wait_recv()
        for place, f in enumerate(group):
            low_end, high_end = (
                jnp.concatenate(
                    [recvs[back][share(back, 2 * n * v + 2 * place + s)] for s in range(2)], axis=0
                )
                for v in range(2)
            )

            def finish_x(i, carry, f=f, place=place, low_end=low_end, high_end=high_end):
                at = rows(pl.multiple_of(f * ROWS + i * NY, NY), NY)
                value = xp[at] + xa[at] * low_end + xb[at] * high_end
                half[at] = value
                low = jnp.sum(ya[at] * value, axis=0, keepdims=True)
                high = jnp.sum(yb[at] * value, axis=0, keepdims=True)
                sends[what][peer_rows(what, i, place, 1)] = low
                sends[what][peer_rows(what, i, n + place, 1)] = high
                return carry

            lax.fori_loop(0, NX, finish_x, 0, unroll=16)
        send(what)
        keep(what)

    def forward(j, right):
        new = []
        for f in range(FIELDS):
            at = y_row(f, j)
            yg[at] = yq[at] * right[f]
            new.append(half[natural(f, j + 1)] + yh[at] * right[f])
        return tuple(new)

    lax.fori_loop(1, NY - 1, forward, tuple(half[natural(f, 1)] for f in range(FIELDS)))

    def backward(k, state):
        j = NY - 2 - k
        new = []
        for f in range(FIELDS):
            at = y_row(f, j)
            p = yg[at] + yh[at] * state[f]
            yp[natural(f, j)] = p
            new.append(p)
        return tuple(new)

    lax.fori_loop(0, NY - 2, backward, (zero,) * FIELDS)

    total("ym").wait_recv()
    y_steps, y_last = [], []
    for g, group in enumerate(GROUPS):
        n = len(group)
        rate_y = rates(group, 1)

        def end_visc(k, v):
            return recvs["ym"][peer_rows("ym", k, 3 * FIELDS + v, 1)]

        def link(j):
            if j % 2 == 0:
                return recvs["ym"][peer_rows("ym", j // 2, y_at[g] + 2 * n)]
            return rate_y * (end_visc(j // 2, 1) + end_visc(j // 2 + 1, 0))

        steps, last = chain_matrix(
            lambda j: recvs["ym"][peer_rows("ym", j // 2, y_at[g] + n * (j % 2))],
            link,
            2.0 * rate_y * end_visc(0, 0),
            2.0 * rate_y * end_visc(PEERS - 1, 1),
            2 * PEERS,
        )
        y_last.append(last)
        y_steps.append([(low, j, high) for low, j, high, *values in steps])
        for low, j, high, *values in steps:
            for kept, value in zip((chain_p, chain_g, chain_h), values):
                if value is not None:
                    kept[rows((2 * g * PEERS + j) * 8, 8)] = value

    for g, group in enumerate(GROUPS):
        what, back, n = ("yr", g), ("yv", g), len(group)
        total(what).wait_recv()
        steps = [
            (low, j, high, *(kept[rows((2 * g * PEERS + j) * 8, 8)] for kept in (chain_p, chain_g, chain_h)))
            for low, j, high in y_steps[g]
        ]
        solved = chain_solve(
            steps, y_last[g], lambda j: recvs[what][peer_rows(what, j // 2, n * (j % 2))], 2 * PEERS
        )
        for k in range(PEERS):
            for v in range(2):
                sends[back][peer_rows(back, k, n * v, n)] = solved[2 * k + v][:n]
        send(back, y_order)
        keep(back)

    for g, group in enumerate(GROUPS):
        back, n = ("yv", g), len(group)
        total(back).wait_recv()

        def finish_y(i, carry):
            for place, f in enumerate(group):
                at = rows(pl.multiple_of(f * ROWS + i * NY, NY), NY)
                low_end = recvs[back][peer_rows(back, i, place, 1)]
                high_end = recvs[back][peer_rows(back, i, n + place, 1)]
                out[at] = yp[at] + ya[at] * low_end + yb[at] * high_end
            return carry

        lax.fori_loop(0, NX, finish_y, 0, unroll=4)
    for what in MESSAGES:
        total(what).wait_send()


def shards(conserved_states, thermal_level, spread_factors):
    def buffer(count):
        return pltpu.VMEM((count, LANES), jnp.float32)

    whole = buffer(FIELDS * ROWS)
    messages = [buffer(PEERS * size) for axis, count, size in MESSAGES.values()]
    arrivals = [buffer(PEERS * size + 8) for axis, count, size in MESSAGES.values()]
    solved = pl.pallas_call(
        kernel,
        out_shape=pltpu.VMEM((FIELDS * ROWS, LANES), jnp.float32),
        in_specs=[
            pl.BlockSpec(memory_space=pl.ANY),
            pl.BlockSpec(memory_space=pl.ANY),
            pl.BlockSpec(memory_space=pl.ANY),
        ],
        out_specs=pl.BlockSpec(memory_space=pltpu.VMEM),
        scratch_shapes=[pltpu.SMEM((FIELDS,), jnp.float32), whole, buffer(ROWS), buffer(ROWS)]
        + [whole] * 13
        + messages
        + arrivals
        + [
            buffer(2 * len(GROUPS) * PEERS * 8),
            buffer(2 * len(GROUPS) * PEERS * 8),
            buffer(2 * len(GROUPS) * PEERS * 8),
            pltpu.SemaphoreType.DMA((len(MESSAGES),)),
            pltpu.SemaphoreType.DMA((len(MESSAGES),)),
            pltpu.SemaphoreType.DMA((3,)),
        ]
        + [pltpu.SemaphoreType.REGULAR] * 2,
        compiler_params=pltpu.CompilerParams(
            collective_id=0, has_side_effects=True, vmem_limit_bytes=60 * 1024 * 1024
        ),
    )(
        conserved_states.reshape(FIELDS * ROWS, LANES),
        thermal_level.reshape(ROWS, LANES),
        spread_factors,
    )
    return solved.reshape(conserved_states.shape)


def solution(mesh):
    return jax.shard_map(
        shards,
        mesh=mesh,
        in_specs=(P(None, "gx", "gy", None), P("gx", "gy", None), P()),
        out_specs=P(None, "gx", "gy", None),
        check_vma=False,
    )
```

```python
import jax
import jax.numpy as jnp
from jax import lax
from jax.experimental import pallas as pl
from jax.experimental.pallas import tpu as pltpu
from jax.sharding import PartitionSpec as P

MESH = pl.DeviceIdType.MESH
FIELDS, NX, NY, LANES = 5, 16, 32, 128
PEERS = 16
ROWS = NX * NY
GROUPS = ((0, 1, 2), (3, 4))


def message_table():
    table = {"ym": ("gy", 3 * FIELDS + 2, 24)}
    for g, group in enumerate(GROUPS):
        n = len(group)
        for name, axis, count in (
            ("xo", "gx", 10 * n + (4 if g == 0 else 0)),
            ("xv", "gx", 4 * n),
            ("yr", "gy", 2 * n),
            ("yv", "gy", 2 * n),
        ):
            table[name, g] = (axis, count, -(-count // 8) * 8)
    return table


MESSAGES = message_table()
ORDER = {what: k for k, what in enumerate(MESSAGES)}

X_STEPS = (
    (2, 2), (2, 1), (1, 2), (2, 3), (3, 2), (1, 1), (1, 3), (3, 1),
    (3, 3), (0, 2), (2, 0), (0, 1), (1, 0), (0, 3), (3, 0),
)
Y_STEPS = (
    (4, 0), (4, 1), (3, 0), (3, 1), (5, 0), (5, 1), (2, 0), (2, 1),
    (6, 0), (6, 1), (1, 0), (1, 1), (7, 0), (7, 1), (0, 1),
)


X_FIRST = tuple(range(16))
Y_FIRST = (1, 3, 9, 5, 8, 2, 7, 11, 4, 10, 6, 13, 15, 12, 0, 14)


def ring(step, size):
    return min(step, size - step)


def others(order, me):
    place = sum(k * (me == at).astype(jnp.int32) for k, at in enumerate(order))
    return [jnp.where(place > k, order[k], order[k + 1]) for k in range(len(order) - 1)]


def partners(axis, gx, gy):
    if axis == "gx":
        return [(((gx + 4 * i) & 12) + ((gx + j) & 3), gy) for i, j in X_STEPS]
    return [(gx, ((gy + 2 * i) & 14) + ((gy + j) & 1)) for i, j in Y_STEPS]


def rows(start, count):
    return pl.ds(start, count)


def chain_matrix(mass, link, wall_low, wall_high, count):
    masses = [mass(j) for j in range(count)]
    links = [link(j) for j in range(count - 1)]
    masses[0] += wall_low
    masses[-1] += wall_high
    nodes, steps = list(range(count)), []
    while len(nodes) > 1:
        fewer = []
        for at in range(1, len(nodes), 2):
            low, j = nodes[at - 1], nodes[at]
            high = nodes[at + 1] if at + 1 < len(nodes) else None
            m, a = masses[j], links[at - 1]
            b = links[at] if high is not None else None
            p = 1.0 / (m + a if high is None else m + (a + b))
            g = a * p
            h = None if high is None else b * p
            steps.append((low, j, high, p, g, h))
            masses[low] += g * m
            if high is not None:
                masses[high] += h * m
                fewer.append(g * b)
        nodes, links = nodes[::2], fewer
    return steps, 1.0 / masses[0]


def chain_solve(steps, last, right, count):
    values = [right(j) for j in range(count)]
    kept = []
    for low, j, high, p, g, h in steps:
        r = values[j]
        kept.append(p * r)
        values[low] += g * r
        if high is not None:
            values[high] += h * r
    values[0] = last * values[0]
    for (low, j, high, p, g, h), q in zip(reversed(steps), reversed(kept)):
        q = q + g * values[low]
        values[j] = q if high is None else q + h * values[high]
    return values


def kernel(
    fields_hbm, level_hbm, spread_hbm, out,
    spread, field, level, visc, xg, xh, xq, xa, xb, xp, half, yg, yh, yq, ya, yb, yp,
    *rest,
):
    gx, gy = lax.axis_index("gx"), lax.axis_index("gy")
    count = len(MESSAGES)
    sends = dict(zip(MESSAGES, rest[:count]))
    recvs = dict(zip(MESSAGES, rest[count : 2 * count]))
    chain_p, chain_g, chain_h, send_sem, recv_sem, in_sem, line_sem, all_sem = rest[2 * count :]
    everyone = partners("gx", gx, gy) + partners("gy", gx, gy)

    front = gx < 4
    my_line = [(((gx + 4 * i) & 12) + (gx & 3), gy) for i in (2, 1, 3)]
    x_partners, y_partners = partners("gx", gx, gy), partners("gy", gx, gy)

    def tell(sem, devices):
        for device in devices:
            pl.semaphore_signal(sem, inc=1, device_id=device, device_id_type=MESH)

    barrier = pltpu.get_barrier_semaphore()
    tell(barrier, x_partners)

    @pl.when(front)
    def _():
        tell(barrier, y_partners)

    level_in = pltpu.make_async_copy(level_hbm, level, in_sem.at[0])
    fields_in = pltpu.make_async_copy(fields_hbm, field, in_sem.at[1])
    spread_in = pltpu.make_async_copy(spread_hbm, spread, in_sem.at[2])
    level_in.start()
    spread_in.start()
    fields_in.start()

    x_order = [(peer, gy) for peer in others(X_FIRST, gx)]
    y_order = [(gx, peer) for peer in others(Y_FIRST, gy)]

    def send(what, devices=None):
        axis, count, size = MESSAGES[what]
        me = gx if axis == "gx" else gy
        for device in devices or partners(axis, gx, gy):
            peer = device[0] if axis == "gx" else device[1]
            pltpu.make_async_remote_copy(
                src_ref=sends[what].at[rows(pl.multiple_of(peer * size, 8), count)],
                dst_ref=recvs[what].at[rows(pl.multiple_of(me * size, 8), count)],
                send_sem=send_sem.at[ORDER[what]],
                recv_sem=recv_sem.at[ORDER[what]],
                device_id=device,
                device_id_type=MESH,
            ).start()

    def keep(what):
        axis, count, size = MESSAGES[what]
        mine = rows(pl.multiple_of((gx if axis == "gx" else gy) * size, 8), size)
        recvs[what][mine] = sends[what][mine]

    def total(what):
        axis, count, size = MESSAGES[what]
        part = rows(0, (PEERS - 1) * count)
        return pltpu.make_async_remote_copy(
            src_ref=sends[what].at[part],
            dst_ref=recvs[what].at[part],
            send_sem=send_sem.at[ORDER[what]],
            recv_sem=recv_sem.at[ORDER[what]],
            device_id=everyone[0],
            device_id_type=MESH,
        )

    def share(what, row):
        return pl.ds(row, PEERS, stride=MESSAGES[what][2])

    def peer_rows(what, k, row, count=8):
        return rows(k * MESSAGES[what][2] + row, count)

    spread_in.wait()
    rate = [2500.0 * spread[f] for f in range(FIELDS)]
    zero = jnp.zeros((16, LANES), jnp.float32)
    one = jnp.ones((16, LANES), jnp.float32)

    for what, (axis, used, size) in MESSAGES.items():
        for row in range(used, size):
            sends[what][share(what, row)] = zero
            recvs[what][share(what, row)] = zero
        recvs[what][rows(PEERS * size, 8)] = zero[:8]

    level_in.wait()

    def power(t, carry):
        at = rows(pl.multiple_of(t * 64, 64), 64)
        visc[at] = jnp.exp(0.7 * jnp.log(level[at]))
        return carry

    lax.fori_loop(0, ROWS // 64, power, 0)
    fields_in.wait()

    def x_row(f, i, s):
        return rows(pl.multiple_of(f * ROWS + i * NY + s * 16, 16), 16)

    def x_visc(i, s):
        return visc[rows(pl.multiple_of(i * NY + s * 16, 16), 16)]

    for s in range(2):
        nu0, nu1 = x_visc(0, s), x_visc(1, s)
        start = (
            nu1,
            tuple(rate[f] * (nu0 + nu1) for f in range(FIELDS)),
            (one,) * FIELDS,
            (one,) * FIELDS,
            tuple(field[x_row(f, 1, s)] for f in range(FIELDS)),
            tuple(field[x_row(f, 0, s)] for f in range(FIELDS)),
        )

        def forward(i, state, s=s):
            nu, edge, mass, first, right, first_right = state
            nu_next = x_visc(i + 1, s)
            face = nu + nu_next
            out_state = ([], [], [], [], [])
            for f in range(FIELDS):
                e, m, r = edge[f], mass[f], right[f]
                w = rate[f] * face
                p = 1.0 / (e + w + m)
                g, h = e * p, w * p
                at = x_row(f, i, s)
                xg[at] = g
                xh[at] = h
                xq[at] = p * r
                for box, item in zip(
                    out_state,
                    (g * w, 1.0 + h * m, first[f] + g * m, field[x_row(f, i + 1, s)] + h * r, first_right[f] + g * r),
                ):
                    box.append(item)
            return (nu_next,) + tuple(tuple(box) for box in out_state)

        nu, edge, mass, first, right, first_right = lax.fori_loop(1, NX - 1, forward, start)
        for g, group in enumerate(GROUPS):
            what, n = ("xo", g), 2 * len(group)
            for place, f in enumerate(group):
                for v, value in enumerate((first[f], mass[f], edge[f], first_right[f], right[f])):
                    sends[what][share(what, v * n + 2 * place + s)] = value
        what, n = ("xo", 0), 10 * len(GROUPS[0])
        sends[what][share(what, n + s)] = nu0
        sends[what][share(what, n + 2 + s)] = nu

    pl.semaphore_wait(barrier, jnp.where(front, len(everyone), len(x_partners)))
    for g in range(len(GROUPS)):
        send(("xo", g))

    @pl.when(front)
    def _():
        tell(line_sem, y_partners)

    for g in range(len(GROUPS)):
        keep(("xo", g))

    def y_visc(j):
        return visc[pl.ds(j, 16, stride=NY)]

    def y_row(f, j):
        return rows(pl.multiple_of((f * NY + j) * 16, 16), 16)

    nu0, nu1 = y_visc(0), y_visc(1)
    start = (nu1, tuple(rate[f] * (nu0 + nu1) for f in range(FIELDS)), (one,) * FIELDS, (one,) * FIELDS)

    def forward(j, state):
        nu, edge, mass, first = state
        nu_next = y_visc(j + 1)
        face = nu + nu_next
        out_state = ([], [], [])
        for f in range(FIELDS):
            e, m = edge[f], mass[f]
            w = rate[f] * face
            p = 1.0 / (e + w + m)
            g, h = e * p, w * p
            at = y_row(f, j)
            yg[at] = g
            yh[at] = h
            yq[at] = p
            for box, item in zip(out_state, (g * w, 1.0 + h * m, first[f] + g * m)):
                box.append(item)
        return (nu_next,) + tuple(tuple(box) for box in out_state)

    nu, edge, mass, first = lax.fori_loop(1, NY - 1, forward, start)
    at = 0
    y_at = []
    for group in GROUPS:
        y_at.append(at)
        for v, values in enumerate((first, mass, edge)):
            for f in group:
                sends["ym"][share("ym", at)] = values[f]
                at += 1
    sends["ym"][share("ym", at)] = nu0
    sends["ym"][share("ym", at + 1)] = nu
    keep("ym")

    for s in range(2):
        for f in range(FIELDS):
            for i, ends in ((0, (one, zero)), (NX - 1, (zero, one))):
                at = x_row(f, i, s)
                xa[at], xb[at], xp[at] = ends[0], ends[1], zero

        def backward(k, state, s=s):
            i = NX - 2 - k
            new = []
            for f in range(FIELDS):
                a, b, p = state[f]
                at = x_row(f, i, s)
                h = xh[at]
                a, b, p = xg[at] + h * a, h * b, xq[at] + h * p
                xa[at], xb[at], xp[at] = a, b, p
                new.append((a, b, p))
            return tuple(new)

        lax.fori_loop(0, NX - 2, backward, ((zero, one, zero),) * FIELDS)

    @pl.when(front)
    def _():
        pl.semaphore_wait(line_sem, len(y_partners))
        tell(all_sem, my_line)

    line = lax.broadcasted_iota(jnp.int32, (8, LANES), 0)

    def rates(group, each):
        value = jnp.full((8, LANES), rate[group[-1]], jnp.float32)
        for place, f in enumerate(group[:-1]):
            value = jnp.where(line // each == place, rate[f], value)
        return value

    for g, group in enumerate(GROUPS):
        what, n = ("xo", g), 2 * len(group)
        rate_x = rates(group, 2)

        def end_visc(k, v):
            base = 10 * len(GROUPS[0]) + 2 * v
            low, high = (recvs["xo", 0][peer_rows(("xo", 0), k, base + s, 1)] for s in range(2))
            return jnp.where(line % 2 == 1, high, low)

        def link(j):
            if j % 2 == 0:
                return recvs[what][peer_rows(what, j // 2, 2 * n)]
            return rate_x * (end_visc(j // 2, 1) + end_visc(j // 2 + 1, 0))

        total(what).wait_recv()
        steps, last = chain_matrix(
            lambda j: recvs[what][peer_rows(what, j // 2, n * (j % 2))],
            link,
            2.0 * rate_x * end_visc(0, 0),
            2.0 * rate_x * end_visc(PEERS - 1, 1),
            2 * PEERS,
        )
        solved = chain_solve(
            steps, last, lambda j: recvs[what][peer_rows(what, j // 2, n * (3 + j % 2))], 2 * PEERS
        )
        back = ("xv", g)
        for k in range(PEERS):
            for v in range(2):
                sends[back][peer_rows(back, k, n * v, n)] = solved[2 * k + v][:n]
        send(back, x_order[:7])
        keep(back)
    for g in range(len(GROUPS)):
        send(("xv", g), x_order[7:])

    @pl.when(jnp.logical_not(front))
    def _():
        pl.semaphore_wait(all_sem, 1)

    send("ym")

    def natural(f, j):
        return pl.ds(f * ROWS + j, 16, stride=NY)

    for f in range(FIELDS):
        for j, ends in ((0, (one, zero)), (NY - 1, (zero, one))):
            at = natural(f, j)
            ya[at], yb[at], yp[at] = ends[0], ends[1], zero

    def backward(k, state):
        j = NY - 2 - k
        new = []
        for f in range(FIELDS):
            a, b = state[f]
            at = y_row(f, j)
            h = yh[at]
            a, b = yg[at] + h * a, h * b
            ya[natural(f, j)], yb[natural(f, j)] = a, b
            new.append((a, b))
        return tuple(new)

    lax.fori_loop(0, NY - 2, backward, ((zero, one),) * FIELDS)

    for g, group in enumerate(GROUPS):
        what, back, n = ("yr", g), ("xv", g), len(group)
        total(back).wait_recv()
        for place, f in enumerate(group):
            low_end, high_end = (
                jnp.concatenate(
                    [recvs[back][share(back, 2 * n * v + 2 * place + s)] for s in range(2)], axis=0
                )
                for v in range(2)
            )

            def finish_x(i, carry, f=f, place=place, low_end=low_end, high_end=high_end):
                at = rows(pl.multiple_of(f * ROWS + i * NY, NY), NY)
                value = xp[at] + xa[at] * low_end + xb[at] * high_end
                half[at] = value
                low = jnp.sum(ya[at] * value, axis=0, keepdims=True)
                high = jnp.sum(yb[at] * value, axis=0, keepdims=True)
                sends[what][peer_rows(what, i, place, 1)] = low
                sends[what][peer_rows(what, i, n + place, 1)] = high
                return carry

            lax.fori_loop(0, NX, finish_x, 0, unroll=16)
        send(what)
        keep(what)

    def forward(j, right):
        new = []
        for f in range(FIELDS):
            at = y_row(f, j)
            yg[at] = yq[at] * right[f]
            new.append(half[natural(f, j + 1)] + yh[at] * right[f])
        return tuple(new)

    lax.fori_loop(1, NY - 1, forward, tuple(half[natural(f, 1)] for f in range(FIELDS)))

    def backward(k, state):
        j = NY - 2 - k
        new = []
        for f in range(FIELDS):
            at = y_row(f, j)
            p = yg[at] + yh[at] * state[f]
            yp[natural(f, j)] = p
            new.append(p)
        return tuple(new)

    lax.fori_loop(0, NY - 2, backward, (zero,) * FIELDS)

    total("ym").wait_recv()
    y_steps, y_last = [], []
    for g, group in enumerate(GROUPS):
        n = len(group)
        rate_y = rates(group, 1)

        def end_visc(k, v):
            return recvs["ym"][peer_rows("ym", k, 3 * FIELDS + v, 1)]

        def link(j):
            if j % 2 == 0:
                return recvs["ym"][peer_rows("ym", j // 2, y_at[g] + 2 * n)]
            return rate_y * (end_visc(j // 2, 1) + end_visc(j // 2 + 1, 0))

        steps, last = chain_matrix(
            lambda j: recvs["ym"][peer_rows("ym", j // 2, y_at[g] + n * (j % 2))],
            link,
            2.0 * rate_y * end_visc(0, 0),
            2.0 * rate_y * end_visc(PEERS - 1, 1),
            2 * PEERS,
        )
        y_last.append(last)
        y_steps.append([(low, j, high) for low, j, high, *values in steps])
        for low, j, high, *values in steps:
            for kept, value in zip((chain_p, chain_g, chain_h), values):
                if value is not None:
                    kept[rows((2 * g * PEERS + j) * 8, 8)] = value

    for g, group in enumerate(GROUPS):
        what, back, n = ("yr", g), ("yv", g), len(group)
        total(what).wait_recv()
        steps = [
            (low, j, high, *(kept[rows((2 * g * PEERS + j) * 8, 8)] for kept in (chain_p, chain_g, chain_h)))
            for low, j, high in y_steps[g]
        ]
        solved = chain_solve(
            steps, y_last[g], lambda j: recvs[what][peer_rows(what, j // 2, n * (j % 2))], 2 * PEERS
        )
        for k in range(PEERS):
            for v in range(2):
                sends[back][peer_rows(back, k, n * v, n)] = solved[2 * k + v][:n]
        send(back, y_order)
        keep(back)

    for g, group in enumerate(GROUPS):
        back, n = ("yv", g), len(group)
        total(back).wait_recv()

        def finish_y(i, carry):
            for place, f in enumerate(group):
                at = rows(pl.multiple_of(f * ROWS + i * NY, NY), NY)
                low_end = recvs[back][peer_rows(back, i, place, 1)]
                high_end = recvs[back][peer_rows(back, i, n + place, 1)]
                out[at] = yp[at] + ya[at] * low_end + yb[at] * high_end
            return carry

        lax.fori_loop(0, NX, finish_y, 0, unroll=4)
    for what in MESSAGES:
        total(what).wait_send()


def shards(conserved_states, thermal_level, spread_factors):
    def buffer(count):
        return pltpu.VMEM((count, LANES), jnp.float32)

    whole = buffer(FIELDS * ROWS + NY)
    messages = [buffer((PEERS + 1) * size) for axis, count, size in MESSAGES.values()]
    arrivals = [buffer((PEERS + 1) * size) for axis, count, size in MESSAGES.values()]
    solved = pl.pallas_call(
        kernel,
        out_shape=pltpu.VMEM((FIELDS * ROWS, LANES), jnp.float32),
        in_specs=[
            pl.BlockSpec(memory_space=pl.ANY),
            pl.BlockSpec(memory_space=pl.ANY),
            pl.BlockSpec(memory_space=pl.ANY),
        ],
        out_specs=pl.BlockSpec(memory_space=pltpu.VMEM),
        scratch_shapes=[pltpu.SMEM((FIELDS,), jnp.float32), buffer(FIELDS * ROWS), buffer(ROWS), buffer(ROWS + NY)]
        + [whole] * 13
        + messages
        + arrivals
        + [
            buffer(2 * len(GROUPS) * PEERS * 8),
            buffer(2 * len(GROUPS) * PEERS * 8),
            buffer(2 * len(GROUPS) * PEERS * 8),
            pltpu.SemaphoreType.DMA((len(MESSAGES),)),
            pltpu.SemaphoreType.DMA((len(MESSAGES),)),
            pltpu.SemaphoreType.DMA((3,)),
        ]
        + [pltpu.SemaphoreType.REGULAR] * 2,
        compiler_params=pltpu.CompilerParams(
            collective_id=0, has_side_effects=True, vmem_limit_bytes=60 * 1024 * 1024
        ),
    )(
        conserved_states.reshape(FIELDS * ROWS, LANES),
        thermal_level.reshape(ROWS, LANES),
        spread_factors,
    )
    return solved.reshape(conserved_states.shape)


def solution(mesh):
    return jax.shard_map(
        shards,
        mesh=mesh,
        in_specs=(P(None, "gx", "gy", None), P("gx", "gy", None), P()),
        out_specs=P(None, "gx", "gy", None),
        check_vma=False,
    )
```

```python
import jax
import jax.numpy as jnp
from jax import lax
from jax.experimental import pallas as pl
from jax.experimental.pallas import tpu as pltpu
from jax.sharding import PartitionSpec as P

MESH = pl.DeviceIdType.MESH
FIELDS, NX, NY, LANES = 5, 16, 32, 128
PEERS = 16
ROWS = NX * NY
GROUPS = ((0, 1, 2), (3, 4))


def message_table():
    table = {"ym": ("gy", 3 * FIELDS + 2, 24)}
    for g, group in enumerate(GROUPS):
        n = len(group)
        for name, axis, count in (
            ("xo", "gx", 10 * n + (4 if g == 0 else 0)),
            ("xv", "gx", 4 * n),
            ("yr", "gy", 2 * n),
            ("yv", "gy", 2 * n),
        ):
            table[name, g] = (axis, count, -(-count // 8) * 8)
    return table


MESSAGES = message_table()
ORDER = {what: k for k, what in enumerate(MESSAGES)}

X_STEPS = (
    (2, 2), (2, 1), (1, 2), (2, 3), (3, 2), (1, 1), (1, 3), (3, 1),
    (3, 3), (0, 2), (2, 0), (0, 1), (1, 0), (0, 3), (3, 0),
)
Y_STEPS = (
    (4, 0), (4, 1), (3, 0), (3, 1), (5, 0), (5, 1), (2, 0), (2, 1),
    (6, 0), (6, 1), (1, 0), (1, 1), (7, 0), (7, 1), (0, 1),
)


X_FIRST = tuple(range(16))
Y_FIRST = (1, 3, 9, 5, 8, 2, 7, 11, 4, 10, 6, 13, 15, 12, 0, 14)


def ring(step, size):
    return min(step, size - step)


def others(order, me):
    place = sum(k * (me == at).astype(jnp.int32) for k, at in enumerate(order))
    return [jnp.where(place > k, order[k], order[k + 1]) for k in range(len(order) - 1)]


def partners(axis, gx, gy):
    if axis == "gx":
        return [(((gx + 4 * i) & 12) + ((gx + j) & 3), gy) for i, j in X_STEPS]
    return [(gx, ((gy + 2 * i) & 14) + ((gy + j) & 1)) for i, j in Y_STEPS]


def rows(start, count):
    return pl.ds(start, count)


def chain_matrix(mass, link, wall_low, wall_high, count):
    masses = [mass(j) for j in range(count)]
    links = [link(j) for j in range(count - 1)]
    masses[0] += wall_low
    masses[-1] += wall_high
    nodes, steps = list(range(count)), []
    while len(nodes) > 1:
        fewer = []
        for at in range(1, len(nodes), 2):
            low, j = nodes[at - 1], nodes[at]
            high = nodes[at + 1] if at + 1 < len(nodes) else None
            m, a = masses[j], links[at - 1]
            b = links[at] if high is not None else None
            p = 1.0 / (m + a if high is None else m + (a + b))
            g = a * p
            h = None if high is None else b * p
            steps.append((low, j, high, p, g, h))
            masses[low] += g * m
            if high is not None:
                masses[high] += h * m
                fewer.append(g * b)
        nodes, links = nodes[::2], fewer
    return steps, 1.0 / masses[0]


def chain_solve(steps, last, right, count):
    values = [right(j) for j in range(count)]
    kept = []
    for low, j, high, p, g, h in steps:
        r = values[j]
        kept.append(p * r)
        values[low] += g * r
        if high is not None:
            values[high] += h * r
    values[0] = last * values[0]
    for (low, j, high, p, g, h), q in zip(reversed(steps), reversed(kept)):
        q = q + g * values[low]
        values[j] = q if high is None else q + h * values[high]
    return values


def kernel(
    fields_hbm, level_hbm, spread_hbm, out,
    spread, field, level, visc, xg, xh, xq, xa, xb, xp, half, yg, yh, yq, ya, yb, yp,
    *rest,
):
    gx, gy = lax.axis_index("gx"), lax.axis_index("gy")
    count = len(MESSAGES)
    sends = dict(zip(MESSAGES, rest[:count]))
    recvs = dict(zip(MESSAGES, rest[count : 2 * count]))
    chain_p, chain_g, chain_h, send_sem, recv_sem, in_sem, line_sem, all_sem = rest[2 * count :]
    everyone = partners("gx", gx, gy) + partners("gy", gx, gy)

    front = gx < 4
    my_line = [(((gx + 4 * i) & 12) + (gx & 3), gy) for i in (2, 1, 3)]
    x_partners, y_partners = partners("gx", gx, gy), partners("gy", gx, gy)

    def tell(sem, devices):
        for device in devices:
            pl.semaphore_signal(sem, inc=1, device_id=device, device_id_type=MESH)

    barrier = pltpu.get_barrier_semaphore()
    tell(barrier, x_partners)

    @pl.when(front)
    def _():
        tell(barrier, y_partners)

    level_in = pltpu.make_async_copy(level_hbm, level, in_sem.at[0])
    fields_in = pltpu.make_async_copy(fields_hbm, field, in_sem.at[1])
    spread_in = pltpu.make_async_copy(spread_hbm, spread, in_sem.at[2])
    level_in.start()
    spread_in.start()
    fields_in.start()

    x_order = [(peer, gy) for peer in others(X_FIRST, gx)]
    y_order = [(gx, peer) for peer in others(Y_FIRST, gy)]

    def send(what, devices=None):
        axis, count, size = MESSAGES[what]
        me = gx if axis == "gx" else gy
        for device in devices or partners(axis, gx, gy):
            peer = device[0] if axis == "gx" else device[1]
            pltpu.make_async_remote_copy(
                src_ref=sends[what].at[rows(pl.multiple_of(peer * size, 8), count)],
                dst_ref=recvs[what].at[rows(pl.multiple_of(me * size, 8), count)],
                send_sem=send_sem.at[ORDER[what]],
                recv_sem=recv_sem.at[ORDER[what]],
                device_id=device,
                device_id_type=MESH,
            ).start()

    def keep(what):
        axis, count, size = MESSAGES[what]
        mine = rows(pl.multiple_of((gx if axis == "gx" else gy) * size, 8), size)
        recvs[what][mine] = sends[what][mine]

    def total(what):
        axis, count, size = MESSAGES[what]
        part = rows(0, (PEERS - 1) * count)
        return pltpu.make_async_remote_copy(
            src_ref=sends[what].at[part],
            dst_ref=recvs[what].at[part],
            send_sem=send_sem.at[ORDER[what]],
            recv_sem=recv_sem.at[ORDER[what]],
            device_id=everyone[0],
            device_id_type=MESH,
        )

    def share(what, row):
        return pl.ds(row, PEERS, stride=MESSAGES[what][2])

    def peer_rows(what, k, row, count=8):
        return rows(k * MESSAGES[what][2] + row, count)

    spread_in.wait()
    rate = [2500.0 * spread[f] for f in range(FIELDS)]
    zero = jnp.zeros((16, LANES), jnp.float32)
    one = jnp.ones((16, LANES), jnp.float32)

    for what, (axis, used, size) in MESSAGES.items():
        for row in range(used, size):
            sends[what][share(what, row)] = zero
            recvs[what][share(what, row)] = zero
        recvs[what][rows(PEERS * size, 8)] = zero[:8]

    level_in.wait()

    def power(t, carry):
        at = rows(pl.multiple_of(t * 64, 64), 64)
        visc[at] = jnp.exp(0.7 * jnp.log(level[at]))
        return carry

    lax.fori_loop(0, ROWS // 64, power, 0)
    fields_in.wait()

    def x_row(f, i, s):
        return rows(pl.multiple_of(f * ROWS + i * NY + s * 16, 16), 16)

    def x_visc(i, s):
        return visc[rows(pl.multiple_of(i * NY + s * 16, 16), 16)]

    for s in range(2):
        nu0, nu1 = x_visc(0, s), x_visc(1, s)
        start = (
            nu1,
            tuple(rate[f] * (nu0 + nu1) for f in range(FIELDS)),
            (one,) * FIELDS,
            (one,) * FIELDS,
            tuple(field[x_row(f, 1, s)] for f in range(FIELDS)),
            tuple(field[x_row(f, 0, s)] for f in range(FIELDS)),
        )

        def forward(i, state, s=s):
            nu, edge, mass, first, right, first_right = state
            nu_next = x_visc(i + 1, s)
            face = nu + nu_next
            out_state = ([], [], [], [], [])
            for f in range(FIELDS):
                e, m, r = edge[f], mass[f], right[f]
                w = rate[f] * face
                p = 1.0 / (e + w + m)
                g, h = e * p, w * p
                at = x_row(f, i, s)
                xg[at] = g
                xh[at] = h
                xq[at] = p * r
                for box, item in zip(
                    out_state,
                    (g * w, 1.0 + h * m, first[f] + g * m, field[x_row(f, i + 1, s)] + h * r, first_right[f] + g * r),
                ):
                    box.append(item)
            return (nu_next,) + tuple(tuple(box) for box in out_state)

        nu, edge, mass, first, right, first_right = lax.fori_loop(1, NX - 1, forward, start)
        for g, group in enumerate(GROUPS):
            what, n = ("xo", g), 2 * len(group)
            for place, f in enumerate(group):
                for v, value in enumerate((first[f], mass[f], edge[f], first_right[f], right[f])):
                    sends[what][share(what, v * n + 2 * place + s)] = value
        what, n = ("xo", 0), 10 * len(GROUPS[0])
        sends[what][share(what, n + s)] = nu0
        sends[what][share(what, n + 2 + s)] = nu

    pl.semaphore_wait(barrier, jnp.where(front, len(everyone), len(x_partners)))
    for g in range(len(GROUPS)):
        send(("xo", g))

    @pl.when(front)
    def _():
        tell(line_sem, y_partners)

    for g in range(len(GROUPS)):
        keep(("xo", g))

    def y_visc(j):
        return visc[pl.ds(j, 16, stride=NY)]

    def y_row(f, j):
        return rows(pl.multiple_of((f * NY + j) * 16, 16), 16)

    nu0, nu1 = y_visc(0), y_visc(1)
    start = (nu1, tuple(rate[f] * (nu0 + nu1) for f in range(FIELDS)), (one,) * FIELDS, (one,) * FIELDS)

    def forward(j, state):
        nu, edge, mass, first = state
        nu_next = y_visc(j + 1)
        face = nu + nu_next
        out_state = ([], [], [])
        for f in range(FIELDS):
            e, m = edge[f], mass[f]
            w = rate[f] * face
            p = 1.0 / (e + w + m)
            g, h = e * p, w * p
            at = y_row(f, j)
            yg[at] = g
            yh[at] = h
            yq[at] = p
            for box, item in zip(out_state, (g * w, 1.0 + h * m, first[f] + g * m)):
                box.append(item)
        return (nu_next,) + tuple(tuple(box) for box in out_state)

    nu, edge, mass, first = lax.fori_loop(1, NY - 1, forward, start)
    at = 0
    y_at = []
    for group in GROUPS:
        y_at.append(at)
        for v, values in enumerate((first, mass, edge)):
            for f in group:
                sends["ym"][share("ym", at)] = values[f]
                at += 1
    sends["ym"][share("ym", at)] = nu0
    sends["ym"][share("ym", at + 1)] = nu
    keep("ym")

    for s in range(2):
        for f in range(FIELDS):
            for i, ends in ((0, (one, zero)), (NX - 1, (zero, one))):
                at = x_row(f, i, s)
                xa[at], xb[at], xp[at] = ends[0], ends[1], zero

        def backward(k, state, s=s):
            i = NX - 2 - k
            new = []
            for f in range(FIELDS):
                a, b, p = state[f]
                at = x_row(f, i, s)
                h = xh[at]
                a, b, p = xg[at] + h * a, h * b, xq[at] + h * p
                xa[at], xb[at], xp[at] = a, b, p
                new.append((a, b, p))
            return tuple(new)

        lax.fori_loop(0, NX - 2, backward, ((zero, one, zero),) * FIELDS)

    @pl.when(front)
    def _():
        pl.semaphore_wait(line_sem, len(y_partners))
        tell(all_sem, my_line)

    line = lax.broadcasted_iota(jnp.int32, (8, LANES), 0)

    def rates(group, each):
        value = jnp.full((8, LANES), rate[group[-1]], jnp.float32)
        for place, f in enumerate(group[:-1]):
            value = jnp.where(line // each == place, rate[f], value)
        return value

    for g, group in enumerate(GROUPS):
        what, n = ("xo", g), 2 * len(group)
        rate_x = rates(group, 2)

        def end_visc(k, v):
            base = 10 * len(GROUPS[0]) + 2 * v
            low, high = (recvs["xo", 0][peer_rows(("xo", 0), k, base + s, 1)] for s in range(2))
            return jnp.where(line % 2 == 1, high, low)

        def link(j):
            if j % 2 == 0:
                return recvs[what][peer_rows(what, j // 2, 2 * n)]
            return rate_x * (end_visc(j // 2, 1) + end_visc(j // 2 + 1, 0))

        total(what).wait_recv()
        steps, last = chain_matrix(
            lambda j: recvs[what][peer_rows(what, j // 2, n * (j % 2))],
            link,
            2.0 * rate_x * end_visc(0, 0),
            2.0 * rate_x * end_visc(PEERS - 1, 1),
            2 * PEERS,
        )
        solved = chain_solve(
            steps, last, lambda j: recvs[what][peer_rows(what, j // 2, n * (3 + j % 2))], 2 * PEERS
        )
        back = ("xv", g)
        for k in range(PEERS):
            for v in range(2):
                sends[back][peer_rows(back, k, n * v, n)] = solved[2 * k + v][:n]
        send(back, x_order[:7])
        keep(back)
    for g in range(len(GROUPS)):
        send(("xv", g), x_order[7:])

    @pl.when(jnp.logical_not(front))
    def _():
        pl.semaphore_wait(all_sem, 1)

    send("ym")

    def natural(f, j):
        return pl.ds(f * ROWS + j, 16, stride=NY)

    for f in range(FIELDS):
        for j, ends in ((0, (one, zero)), (NY - 1, (zero, one))):
            at = natural(f, j)
            ya[at], yb[at], yp[at] = ends[0], ends[1], zero

    def backward(k, state):
        j = NY - 2 - k
        new = []
        for f in range(FIELDS):
            a, b = state[f]
            at = y_row(f, j)
            h = yh[at]
            a, b = yg[at] + h * a, h * b
            ya[natural(f, j)], yb[natural(f, j)] = a, b
            new.append((a, b))
        return tuple(new)

    lax.fori_loop(0, NY - 2, backward, ((zero, one),) * FIELDS)

    for g, group in enumerate(GROUPS):
        what, back, n = ("yr", g), ("xv", g), len(group)
        total(back).wait_recv()
        for place, f in enumerate(group):
            low_end, high_end = (
                jnp.concatenate(
                    [recvs[back][share(back, 2 * n * v + 2 * place + s)] for s in range(2)], axis=0
                )
                for v in range(2)
            )

            def finish_x(i, carry, f=f, place=place, low_end=low_end, high_end=high_end):
                at = rows(pl.multiple_of(f * ROWS + i * NY, NY), NY)
                value = xp[at] + xa[at] * low_end + xb[at] * high_end
                half[at] = value
                low = jnp.sum(ya[at] * value, axis=0, keepdims=True)
                high = jnp.sum(yb[at] * value, axis=0, keepdims=True)
                sends[what][peer_rows(what, i, place, 1)] = low
                sends[what][peer_rows(what, i, n + place, 1)] = high
                return carry

            lax.fori_loop(0, NX, finish_x, 0, unroll=16)
        send(what)
        keep(what)

    def forward(j, right):
        new = []
        for f in range(FIELDS):
            at = y_row(f, j)
            yg[at] = yq[at] * right[f]
            new.append(half[natural(f, j + 1)] + yh[at] * right[f])
        return tuple(new)

    lax.fori_loop(1, NY - 1, forward, tuple(half[natural(f, 1)] for f in range(FIELDS)))

    def backward(k, state):
        j = NY - 2 - k
        new = []
        for f in range(FIELDS):
            at = y_row(f, j)
            p = yg[at] + yh[at] * state[f]
            yp[natural(f, j)] = p
            new.append(p)
        return tuple(new)

    lax.fori_loop(0, NY - 2, backward, (zero,) * FIELDS)

    total("ym").wait_recv()
    y_steps, y_last = [], []
    for g, group in enumerate(GROUPS):
        n = len(group)
        rate_y = rates(group, 1)

        def end_visc(k, v):
            return recvs["ym"][peer_rows("ym", k, 3 * FIELDS + v, 1)]

        def link(j):
            if j % 2 == 0:
                return recvs["ym"][peer_rows("ym", j // 2, y_at[g] + 2 * n)]
            return rate_y * (end_visc(j // 2, 1) + end_visc(j // 2 + 1, 0))

        steps, last = chain_matrix(
            lambda j: recvs["ym"][peer_rows("ym", j // 2, y_at[g] + n * (j % 2))],
            link,
            2.0 * rate_y * end_visc(0, 0),
            2.0 * rate_y * end_visc(PEERS - 1, 1),
            2 * PEERS,
        )
        y_last.append(last)
        y_steps.append([(low, j, high) for low, j, high, *values in steps])
        for low, j, high, *values in steps:
            for kept, value in zip((chain_p, chain_g, chain_h), values):
                if value is not None:
                    kept[rows((2 * g * PEERS + j) * 8, 8)] = value

    for g, group in enumerate(GROUPS):
        what, back, n = ("yr", g), ("yv", g), len(group)
        total(what).wait_recv()
        steps = [
            (low, j, high, *(kept[rows((2 * g * PEERS + j) * 8, 8)] for kept in (chain_p, chain_g, chain_h)))
            for low, j, high in y_steps[g]
        ]
        solved = chain_solve(
            steps, y_last[g], lambda j: recvs[what][peer_rows(what, j // 2, n * (j % 2))], 2 * PEERS
        )
        for k in range(PEERS):
            for v in range(2):
                sends[back][peer_rows(back, k, n * v, n)] = solved[2 * k + v][:n]
        send(back, y_order[:1])
        keep(back)
    for g in range(len(GROUPS)):
        send(("yv", g), y_order[1:])

    for g, group in enumerate(GROUPS):
        back, n = ("yv", g), len(group)
        total(back).wait_recv()

        def finish_y(i, carry):
            for place, f in enumerate(group):
                at = rows(pl.multiple_of(f * ROWS + i * NY, NY), NY)
                low_end = recvs[back][peer_rows(back, i, place, 1)]
                high_end = recvs[back][peer_rows(back, i, n + place, 1)]
                out[at] = yp[at] + ya[at] * low_end + yb[at] * high_end
            return carry

        lax.fori_loop(0, NX, finish_y, 0, unroll=4)
    for what in MESSAGES:
        total(what).wait_send()


def shards(conserved_states, thermal_level, spread_factors):
    def buffer(count):
        return pltpu.VMEM((count, LANES), jnp.float32)

    whole = buffer(FIELDS * ROWS + NY)
    messages = [buffer((PEERS + 1) * size) for axis, count, size in MESSAGES.values()]
    arrivals = [buffer((PEERS + 1) * size) for axis, count, size in MESSAGES.values()]
    solved = pl.pallas_call(
        kernel,
        out_shape=pltpu.VMEM((FIELDS * ROWS, LANES), jnp.float32),
        in_specs=[
            pl.BlockSpec(memory_space=pl.ANY),
            pl.BlockSpec(memory_space=pl.ANY),
            pl.BlockSpec(memory_space=pl.ANY),
        ],
        out_specs=pl.BlockSpec(memory_space=pltpu.VMEM),
        scratch_shapes=[pltpu.SMEM((FIELDS,), jnp.float32), buffer(FIELDS * ROWS), buffer(ROWS), buffer(ROWS + NY)]
        + [whole] * 13
        + messages
        + arrivals
        + [
            buffer(2 * len(GROUPS) * PEERS * 8),
            buffer(2 * len(GROUPS) * PEERS * 8),
            buffer(2 * len(GROUPS) * PEERS * 8),
            pltpu.SemaphoreType.DMA((len(MESSAGES),)),
            pltpu.SemaphoreType.DMA((len(MESSAGES),)),
            pltpu.SemaphoreType.DMA((3,)),
        ]
        + [pltpu.SemaphoreType.REGULAR] * 2,
        compiler_params=pltpu.CompilerParams(
            collective_id=0, has_side_effects=True, vmem_limit_bytes=60 * 1024 * 1024
        ),
    )(
        conserved_states.reshape(FIELDS * ROWS, LANES),
        thermal_level.reshape(ROWS, LANES),
        spread_factors,
    )
    return solved.reshape(conserved_states.shape)


def solution(mesh):
    return jax.shard_map(
        shards,
        mesh=mesh,
        in_specs=(P(None, "gx", "gy", None), P("gx", "gy", None), P()),
        out_specs=P(None, "gx", "gy", None),
        check_vma=False,
    )
```
